256 devices in a mesh: gx: 16 (over x_hi, z), gy: 4 (over x_lo, core), gz: 4 (over y).
Axes of the slice: x: 4 (x_hi: 2, x_lo: 2; x = x_hi * 2 + x_lo), y: 4, z: 8, core: 2. Of those that a mesh axis runs over, the one named last changes fastest.
Arguments:
- fine_params: float32 [16, 8, 8, 8704], P('gx', 'gy', 'gz'), may hold values from -0.75 to 0.75
- coarse_inner: float32 [5, 512], replicated, may hold values from -4 to 4
- coarse_outer: float32 [512], replicated, may hold values from -0.25 to 0.25
- points: float32 [16, 8, 8, 4, 128], P('gx', 'gy', 'gz'), may hold values from -1 to 1
- source: float32 [16, 8, 8, 128], P('gx', 'gy', 'gz'), may hold values from -6 to 6
- conductivity: float32 [16, 8, 8], P('gx', 'gy', 'gz'), may hold values from 0.3 to 3
- face_points: int32 [16, 8, 8, 6, 32], P('gx', 'gy', 'gz'), may hold values from 0 to 127, as said below
Outputs:
- residual: float32 [16, 8, 8, 128], P('gx', 'gy', 'gz')
- fine_grads: float32 [16, 8, 8, 8704], P('gx', 'gy', 'gz')
- coarse_inner_grads: float32 [5, 512], replicated
- coarse_outer_grads: float32 [512], replicated
The draws below stay inside these ranges and needn't reach their ends.
Inputs may be any that keep to these rules, and one draw needn't show every extreme that they name: Each row face_points[a, b, c, d, :] holds 32 distinct point numbers.
All inputs are finite; a program needn't handle non-finite values.
Results may differ from the reference program's by a relative error of at most 0.0003.
Values sent between devices are 32-bit elements; how exact they have to be, the bound alone decides.
A program may use at most 192 MiB of HBM per device.

```python
import math
from functools import partial
import jax
import jax.numpy as jnp
from jax import lax

PTS = 128
FACE = 32
HID = 64
COARSE = 512
NPAR = 8704
NSX = 16
NSY = 8
NSZ = 8
SUBDOMAINS = 1024


def draw_face_points(key, part):
    key = jax.random.fold_in(key, 7)
    scores = jax.random.randint(key, (NSX, NSY, NSZ, 6, PTS), 0, 1 << 20) * PTS + jnp.arange(PTS, dtype=jnp.int32)
    ranking = jnp.argsort(scores, axis=-1)
    return ranking[..., 0:FACE].astype(jnp.int32)


def level_of(key, extent, shards, low, high):
    factor_of = 1.0
    for dim, blocks in shards:
        steps = jax.random.uniform(jax.random.fold_in(jax.random.fold_in(key, 6), dim), (blocks,), jnp.float32, low / len(shards), high / len(shards))
        factor_of = factor_of * jnp.repeat(jnp.exp(steps), extent[dim] // blocks).reshape((-1,) + (1,) * (len(extent) - 1 - dim))
    return factor_of


def bell_draw(stream_key, extent, deviation, reach, pieces=(), held_as=jnp.bfloat16):
    level = level_of(stream_key, extent, pieces, -0.22, 0.18) if pieces else 1.0
    values = jax.random.normal(stream_key, extent, jnp.float32) * deviation * level
    return jnp.minimum(jnp.maximum(values, -reach), reach).astype(held_as)


def setup_inputs(seed: int = 0) -> dict:
    key_of = jax.random.split(jax.random.key(seed), 8)
    fine_params = bell_draw(key_of[0], (NSX, NSY, NSZ, NPAR), HID ** -0.5, 0.75, ((0, 16), (1, 4), (2, 4)), jnp.float32)
    coarse_inner = bell_draw(key_of[1], (5, COARSE), 1.0, 4.0, (), jnp.float32)
    coarse_outer = bell_draw(key_of[2], (COARSE,), COARSE ** -0.5, 0.25, (), jnp.float32)
    points = jnp.clip(jax.random.uniform(key_of[3], (NSX, NSY, NSZ, 4, PTS), jnp.float32, -1.0, 1.0) * level_of(key_of[3], (NSX, NSY, NSZ, 4, PTS), ((0, 16), (1, 4), (2, 4)), -0.4, 0.0), -1.0, 1.0)
    source = bell_draw(key_of[4], (NSX, NSY, NSZ, PTS), 1.0, 6.0, ((0, 16), (1, 4), (2, 4)), jnp.float32)
    conductivity = jnp.clip(jnp.exp(math.log(3.0) - 2.3025851 * jax.random.uniform(key_of[5], (NSX, NSY, NSZ), jnp.float32) ** level_of(key_of[5], (NSX, NSY, NSZ), ((0, 16), (1, 4), (2, 4)), -0.2, 0.2)), 0.3, 3.0)
    face_points = draw_face_points(jax.random.fold_in(key_of[7], 71), 0)
    return dict(fine_params=fine_params, coarse_inner=coarse_inner, coarse_outer=coarse_outer, points=points, source=source, conductivity=conductivity, face_points=face_points)


exact_mode = lax.Precision.HIGHEST

def int_starts(values):
    return tuple((jnp.asarray(value).astype(jnp.int32) for value in values))

def unpack(params):
    batch_rows = params.shape[0]
    layer_one = params[:, 0:4 * HID].reshape(batch_rows, 4, HID)
    cursor = 4 * HID
    bias_one = params[:, cursor:cursor + HID]
    cursor = cursor + HID
    layer_two = params[:, cursor:cursor + HID * HID].reshape(batch_rows, HID, HID)
    cursor = cursor + HID * HID
    bias_two = params[:, cursor:cursor + HID]
    cursor = cursor + HID
    layer_three = params[:, cursor:cursor + HID * HID].reshape(batch_rows, HID, HID)
    cursor = cursor + HID * HID
    bias_three = params[:, cursor:cursor + HID]
    cursor = cursor + HID
    out_vector = params[:, cursor:cursor + HID]
    return (layer_one, bias_one, layer_two, bias_two, layer_three, bias_three, out_vector)

def activate(pre_act):
    hidden = jnp.tanh(pre_act)
    slope_one = 1.0 - hidden * hidden
    return (hidden, slope_one, -2.0 * hidden * slope_one)

def network(params, inputs):
    layer_one, bias_one, layer_two, bias_two, layer_three, bias_three, out_vector = unpack(params)
    batch_rows = inputs.shape[0]
    points_count = inputs.shape[2]
    pre_act = jnp.einsum('bih,biq->bhq', layer_one, inputs, precision=exact_mode) + bias_one[:, :, None]
    hidden, slope_one, slope_two = activate(pre_act)
    columns = jnp.swapaxes(layer_one, 1, 2)[:, :, :, None]
    firsts = slope_one[:, :, None, :] * columns
    seconds = slope_two[:, :, None, :] * columns[:, :, 0:3, :] * columns[:, :, 0:3, :]
    stacked = jnp.concatenate([hidden[:, :, None, :], firsts, seconds], axis=2)
    for weights, biases in ((layer_two, bias_two), (layer_three, bias_three)):
        flattened = stacked.reshape(batch_rows, HID, 8 * points_count)
        product = jnp.einsum('bhk,bhn->bkn', weights, flattened, precision=exact_mode)
        product = product.reshape(batch_rows, HID, 8, points_count)
        hidden, slope_one, slope_two = activate(product[:, :, 0, :] + biases[:, :, None])
        firsts = slope_one[:, :, None, :] * product[:, :, 1:5, :]
        seconds = slope_two[:, :, None, :] * product[:, :, 1:4, :] * product[:, :, 1:4, :] + slope_one[:, :, None, :] * product[:, :, 5:8, :]
        stacked = jnp.concatenate([hidden[:, :, None, :], firsts, seconds], axis=2)
    flattened = stacked.reshape(batch_rows, HID, 8 * points_count)
    return jnp.einsum('bh,bhn->bn', out_vector, flattened, precision=exact_mode).reshape(batch_rows, 8, points_count)

def windowed(channels, inputs):
    spatial = inputs[:, 0:3, :]
    window = jnp.exp(-lax.optimization_barrier(jnp.sum(spatial * spatial, axis=1)))
    slopes = -2.0 * spatial * window[:, None, :]
    curves = (4.0 * spatial * spatial - 2.0) * window[:, None, :]
    time_rate = 2.0 * window * channels[:, 4, :]
    spread = lax.optimization_barrier(jnp.sum(curves * channels[:, 0:1, :] + 2.0 * slopes * channels[:, 1:4, :] + window[:, None, :] * channels[:, 5:8, :], axis=1))
    return jnp.stack([time_rate, spread], axis=1)

def coarse_terms(coarse_inner, coarse_outer, places, time_inputs, scales):
    inputs = jnp.stack([places[0] * scales[0] - 1.0, places[1] * scales[1] - 1.0, places[2] * scales[2] - 1.0, time_inputs])
    pre_act = jnp.dot(jnp.transpose(coarse_inner[0:4]), inputs, precision=exact_mode) + coarse_inner[4][:, None]
    hidden, slope_one, slope_two = activate(pre_act)
    time_rate = 2.0 * jnp.dot(coarse_outer * coarse_inner[3], slope_one, precision=exact_mode)
    curvature = coarse_outer * (coarse_inner[0] * coarse_inner[0] * (scales[0] * scales[0]) + coarse_inner[1] * coarse_inner[1] * (scales[1] * scales[1]) + coarse_inner[2] * coarse_inner[2] * (scales[2] * scales[2]))
    spread = jnp.dot(curvature, slope_two, precision=exact_mode)
    return (time_rate, spread)

def assemble(own_channels, face_channels, coarse_inner, coarse_outer, coords, onehots, face_inputs, source_rows, diffusivity, places, scales):
    summed = windowed(own_channels, coords)
    for direction in range(6):
        added = windowed(face_channels[direction], face_inputs[direction])
        summed = summed + jnp.einsum('sfp,scf->scp', onehots[:, direction], added, precision=exact_mode)
    coarse_rate, coarse_spread = coarse_terms(coarse_inner, coarse_outer, places, coords[:, 3, :].reshape(-1), scales)
    grid_shape = source_rows.shape
    time_rate = summed[:, 0, :] + coarse_rate.reshape(grid_shape)
    spread = summed[:, 1, :] + coarse_spread.reshape(grid_shape)
    residual = time_rate - diffusivity[:, None] * spread - source_rows
    return (0.5 * jnp.sum(residual * residual) / PTS, residual)

def reference(fine_params, coarse_inner, coarse_outer, points, source, conductivity, face_points):
    padded = jnp.pad(fine_params, ((1, 1), (1, 1), (1, 1), (0, 0)))
    param_count = fine_params.shape[3]
    slab_count = NSY * NSZ
    scales = (2.0 / NSX, 2.0 / NSY, 2.0 / NSZ)
    cross_grid = jnp.indices((NSY, NSZ)).reshape(2, slab_count).astype(jnp.float32) + 0.5

    def slab_terms(padded_all, inner_params, outer_params, position):
        position = position.astype(jnp.int32)
        own_params = lax.dynamic_slice(padded_all, int_starts((position + 1, 1, 1, 0)), (1, NSY, NSZ, param_count)).reshape(slab_count, param_count)
        coords = lax.dynamic_slice(points, int_starts((position, 0, 0, 0, 0)), (1, NSY, NSZ, 4, PTS)).reshape(slab_count, 4, PTS)
        face_rows = lax.dynamic_slice(face_points, int_starts((position, 0, 0, 0, 0)), (1, NSY, NSZ, 6, FACE)).reshape(slab_count, 6, FACE)
        source_rows = lax.dynamic_slice(source, int_starts((position, 0, 0, 0)), (1, NSY, NSZ, PTS)).reshape(slab_count, PTS)
        diffusivity = lax.dynamic_slice(conductivity, int_starts((position, 0, 0)), (1, NSY, NSZ)).reshape(slab_count)
        onehots = (face_rows[..., None] == jnp.arange(PTS, dtype=jnp.int32)).astype(jnp.float32)
        first_row = jnp.zeros((1, slab_count), jnp.float32) + position.astype(jnp.float32) + 0.5
        centres = jnp.concatenate([first_row, cross_grid], axis=0)
        places = (centres[:, :, None] + jnp.swapaxes(coords[:, 0:3, :], 0, 1)).reshape(3, slab_count * PTS)
        face_inputs = []
        face_channels = []
        for direction in range(6):
            axis_number = direction // 2
            step_sign = 2 * (direction % 2) - 1
            starts = [position + 1, 1, 1]
            starts[axis_number] = starts[axis_number] + step_sign
            neighbour_block = lax.dynamic_slice(padded_all, int_starts((starts[0], starts[1], starts[2], 0)), (1, NSY, NSZ, param_count))
            gathered = jnp.einsum('sfp,scp->scf', onehots[:, direction], coords, precision=exact_mode)
            unit_shift = (jnp.arange(4) == axis_number).astype(jnp.float32) * step_sign
            shifted = gathered - unit_shift[None, :, None]
            face_inputs.append(shifted)
            face_channels.append(network(neighbour_block.reshape(slab_count, param_count), shifted))
        own_channels = network(own_params, coords)
        return assemble(own_channels, tuple(face_channels), inner_params, outer_params, coords, onehots, tuple(face_inputs), source_rows, diffusivity, places, scales)

    def objective(padded_all, inner_params, outer_params):
        losses, residuals = lax.map(jax.checkpoint(partial(slab_terms, padded_all, inner_params, outer_params)), jnp.arange(NSX, dtype=jnp.int32))
        return (jnp.sum(losses), residuals)
    gradients, residuals = jax.grad(objective, argnums=(0, 1, 2), has_aux=True)(padded, coarse_inner, coarse_outer)
    factor = SUBDOMAINS ** (-0.5)
    return (residuals.reshape(NSX, NSY, NSZ, PTS), gradients[0][1:-1, 1:-1, 1:-1], gradients[1] * factor, gradients[2] * factor)
```

```python
from functools import partial

import jax
import jax.numpy as jnp
from jax import lax
from jax.experimental import pallas as pl
from jax.experimental.pallas import tpu as pltpu
from jax.sharding import PartitionSpec as P

PTS = 128
FACE = 32
HID = 64
COARSE = 512
ROWS = 68
NETS = 4
CH = 6
WIDTH = CH * PTS
AXES = ("gx", "gy", "gz")
MESH = pl.DeviceIdType.MESH
BF = jnp.bfloat16
F32 = jnp.float32


def split2(x):
    hi = x.astype(BF)
    return hi, (x - hi.astype(F32)).astype(BF)


def split3(x):
    hi = x.astype(BF)
    rest = x - hi.astype(F32)
    mid = rest.astype(BF)
    return hi, mid, (rest - mid.astype(F32)).astype(BF)


def dot(a, b):
    return lax.dot_general(a, b, (((1,), (0,)), ((), ())), preferred_element_type=F32)


def dot_nt(a, b):
    return lax.dot_general(a, b, (((1,), (1,)), ((), ())), preferred_element_type=F32)


def iota(shape, dim):
    return lax.broadcasted_iota(jnp.int32, shape, dim)


def stacked3(row):
    which = iota((16, row.shape[1]), 0)
    hi = row.astype(BF).astype(F32)
    rest = row - hi
    mid = rest.astype(BF).astype(F32)
    low = rest - mid
    rows = jnp.where(which == 0, hi, jnp.where(which == 1, mid, jnp.where(which == 2, low, 0.0)))
    return rows.astype(BF)


def coefficients(x):
    sx, sy, sz, kappa = x[0:1], x[1:2], x[2:3], x[4:5]
    square = sx * sx + sy * sy + sz * sz
    window = jnp.exp(-square)
    scaled = kappa * window
    return (
        scaled * (6.0 - 4.0 * square),
        4.0 * scaled * sx,
        4.0 * scaled * sy,
        4.0 * scaled * sz,
        2.0 * window,
        -scaled,
    )


def kernel(
    sizes,
    params,
    inner,
    outer,
    points,
    source,
    kappa,
    faces,
    res_out,
    grad_out,
    coarse_out,
    hot,
    gbuf,
    gin,
    ebuf,
    ein,
    rbuf,
    rin,
    xs,
    cols,
    wide,
    wsq,
    lf,
    lb,
    act1,
    act2,
    hid1,
    state2,
    dlast,
    qs,
    dz,
    acc3,
    acc2,
    acc1,
    acco,
    work,
    eown,
    ecoarse,
    ccols,
    cact,
    cvec,
    ar,
    g_send,
    g_recv,
    e_send,
    e_recv,
    r_send,
    r_recv,
    ar_send,
    ar_recv,
):
    place = [lax.axis_index(axis) for axis in AXES]

    def target(slot, flip):
        axis = slot // 2
        sign = (2 * (slot % 2) - 1) * (-1 if flip else 1)
        return AXES[axis], place[axis] + sign, sizes[axis]

    low = min(4, sizes[0])
    groups = [
        ("gy", place[1], sizes[1], lambda p: p),
        ("gz", place[2], sizes[2], lambda p: p),
        ("gx", place[0] % low, low, lambda p: (place[0] // low) * low + p),
        ("gx", place[0] // low, sizes[0] // low, lambda p: p * low + place[0] % low),
    ]

    def exchange(source_of, landing, send_sem, recv_sem, flip):
        for slot in range(6):
            axis, where, size = target(slot, flip)

            @pl.when(jnp.logical_and(where >= 0, where < size))
            def _(slot=slot, axis=axis, where=where):
                pltpu.make_async_remote_copy(
                    source_of(slot), landing.at[slot], send_sem.at[slot], recv_sem.at[slot],
                    device_id={axis: where}, device_id_type=MESH,
                ).start()

    def arrive(source_of, landing, send_sem, recv_sem, flip):
        for slot in range(6):
            axis, where, size = target(slot, not flip)

            @pl.when(jnp.logical_and(where >= 0, where < size))
            def _(slot=slot, axis=axis, where=where):
                pltpu.make_async_remote_copy(
                    source_of(slot), landing.at[slot], send_sem.at[slot], recv_sem.at[slot],
                    device_id={axis: where}, device_id_type=MESH,
                ).wait_recv()

    def sent(source_of, landing, send_sem, recv_sem, flip):
        for slot in range(6):
            axis, where, size = target(slot, flip)

            @pl.when(jnp.logical_and(where >= 0, where < size))
            def _(slot=slot, axis=axis, where=where):
                pltpu.make_async_remote_copy(
                    source_of(slot), landing.at[slot], send_sem.at[slot], recv_sem.at[slot],
                    device_id={axis: where}, device_id_type=MESH,
                ).wait_send()

    def ar_copies(stage, arriving):
        axis, pos, size, member = groups[stage]
        for k in range(1, size):
            partner = lax.rem(pos + k, size)
            slot = partner if arriving else pos
            yield pltpu.make_async_remote_copy(
                ar.at[stage, pos], ar.at[stage, slot],
                ar_send.at[stage, partner], ar_recv.at[stage, slot],
                device_id={axis: member(partner)}, device_id_type=MESH,
            )

    def ar_start(stage, value):
        ar[stage, groups[stage][1]] = value
        for out in ar_copies(stage, False):
            out.start()

    def ar_finish(stage):
        for back in ar_copies(stage, True):
            back.wait_recv()
        total = ar[stage, 0]
        for p in range(1, groups[stage][2]):
            total = total + ar[stage, p]
        return total

    gin[...] = jnp.zeros_like(gin)
    ein[...] = jnp.zeros_like(ein)
    rin[...] = jnp.zeros_like(rin)

    barrier = pltpu.get_barrier_semaphore()
    expected = 0
    for slot in (0, 1):
        axis, where, size = target(slot, False)
        present = jnp.logical_and(where >= 0, where < size)

        @pl.when(present)
        def _(axis=axis, where=where):
            pl.semaphore_signal(barrier, inc=1, device_id={axis: where}, device_id_type=MESH)

        expected = expected + jnp.where(present, 1, 0)
    for axis, pos, size, member in groups:
        for k in range(1, size):
            pl.semaphore_signal(
                barrier, inc=1, device_id={axis: member(lax.rem(pos + k, size))}, device_id_type=MESH
            )
        expected = expected + (size - 1)

    lane = iota((1, PTS), 1)
    row8 = iota((8, PTS), 0)
    group = lane // FACE
    for j in range(NETS):
        b, c = j // 2, j % 2
        index = faces[j]
        first = jnp.concatenate([index[k : k + 1] for k in range(4)], axis=1)
        second = jnp.concatenate(
            [index[4:5], index[5:6], jnp.full((1, 2 * FACE), -1, jnp.int32)], axis=1
        )
        point = iota((PTS, PTS), 0)
        hot[j, :, 0:PTS] = jnp.where(point == first, 1.0, 0.0).astype(BF)
        hot[j, :, PTS : 2 * PTS] = jnp.where(point == second, 1.0, 0.0).astype(BF)
        own = jnp.concatenate([points[j], jnp.zeros((4, PTS), F32)], axis=0)
        own = jnp.where(row8 == 4, kappa[b, c], own)
        xs[j, 0] = own
        hi, mid, low_part = split3(own)
        pieces = jnp.concatenate([hi, mid, low_part, jnp.zeros_like(hi)], axis=0)
        moved = dot(pieces, hot[j])
        moved = moved[0:8] + moved[8:16] + moved[16:24]
        shift_a = jnp.where(row8 == group // 2, (2 * (group % 2) - 1).astype(F32), 0.0)
        shift_b = jnp.where(row8 == 2, jnp.where(group < 2, (2 * (group % 2) - 1).astype(F32), 0.0), 0.0)
        gbuf[0, j] = moved[:, 0:PTS] - shift_a
        gbuf[1, j] = moved[:, PTS : 2 * PTS] - shift_b

    pl.semaphore_wait(barrier, expected)
    g_args = (lambda slot: gbuf.at[slot // 4], gin, g_send, g_recv, False)
    exchange(*g_args)

    half = iota((32, PTS), 1) < HID
    for n in range(NETS):
        flat = params[n]
        even = pltpu.roll(jnp.where(half, flat[35:67], flat[2:34]), HID, 1)
        odd = jnp.where(half, flat[3:35], flat[35:67])
        work[pl.ds(0, 32, stride=2), :] = even
        work[pl.ds(1, 32, stride=2), :] = odd
        both = work[...]
        hi, lo = split2(both)
        lb[n, 0, :, 0:64] = hi[:, 0:64]
        lb[n, 0, :, 64:128] = hi[:, 0:64]
        lb[n, 0, :, 128:192] = lo[:, 0:64]
        lb[n, 1, :, 0:64] = hi[:, 64:128]
        lb[n, 1, :, 64:128] = hi[:, 64:128]
        lb[n, 1, :, 128:192] = lo[:, 64:128]
        hi, lo = split2(both.T)
        for layer in range(2):
            lf[n, layer, :, 0:64] = hi[64 * layer : 64 * layer + 64]
            lf[n, layer, :, 64:128] = hi[64 * layer : 64 * layer + 64]
            lf[n, layer, :, 128:192] = lo[64 * layer : 64 * layer + 64]
        vectors = jnp.concatenate(
            [
                flat[0:1],
                pltpu.roll(flat[0:1], HID, 1),
                flat[1:2],
                pltpu.roll(flat[1:2], HID, 1),
                flat[2:3],
                pltpu.roll(flat[34:35], HID, 1),
                flat[67:68],
                pltpu.roll(flat[67:68], HID, 1),
            ],
            axis=0,
        )
        columns = vectors.T
        for k in range(8):
            wide[n, k] = jnp.broadcast_to(columns[0:64, k : k + 1], (64, PTS))
        wsq[n] = wide[n, 0] * wide[n, 0] + wide[n, 1] * wide[n, 1] + wide[n, 2] * wide[n, 2]
        first_channel = jnp.where(
            jnp.logical_and(iota((16, PTS), 0) == 0, iota((16, PTS), 1) >= 0), 1.0, 0.0
        ).astype(BF)
        for tile in range(3):
            for k in range(CH):
                at = (tile * CH + k) * PTS
                value = first_channel if k == 0 else jnp.zeros_like(first_channel)
                act1[n, 192:208, at : at + PTS] = value
                act2[n, 192:208, at : at + PTS] = value

    def put(ref, n, at, value):
        hi, lo = split2(value)
        ref[n, 0:64, at : at + PTS] = hi
        ref[n, 64:128, at : at + PTS] = lo
        ref[n, 128:192, at : at + PTS] = hi

    def forward(n, tiles):
        begin, end = tiles[0] * WIDTH, (tiles[-1] + 1) * WIDTH
        for tile in tiles:
            x = xs[n, tile]
            pre = (
                wide[n, 4]
                + wide[n, 0] * x[0:1]
                + wide[n, 1] * x[1:2]
                + wide[n, 2] * x[2:3]
                + wide[n, 3] * x[3:4]
            )
            hidden = jnp.tanh(pre)
            one = 1.0 - hidden * hidden
            two = -2.0 * hidden * one
            hid1[n, :, tile * PTS : (tile + 1) * PTS] = hidden
            at = tile * WIDTH
            put(act1, n, at, hidden)
            for k in range(4):
                put(act1, n, at + (k + 1) * PTS, one * wide[n, k])
            put(act1, n, at + 5 * PTS, two * wsq[n])
        product = dot(lf[n, 0], act1[n, 0:192, begin:end])
        for tile in tiles:
            at = tile * WIDTH
            z = [product[:, at - begin + k * PTS : at - begin + (k + 1) * PTS] for k in range(CH)]
            hidden = jnp.tanh(z[0] + wide[n, 5])
            one = 1.0 - hidden * hidden
            two = -2.0 * hidden * one
            state2[n, :, at : at + PTS] = hidden
            for k in range(1, CH):
                state2[n, :, at + k * PTS : at + (k + 1) * PTS] = z[k]
            put(act2, n, at, hidden)
            for k in range(1, 5):
                put(act2, n, at + k * PTS, one * z[k])
            put(act2, n, at + 5 * PTS, two * (z[1] * z[1] + z[2] * z[2] + z[3] * z[3]) + one * z[5])
        product = dot(lf[n, 1], act2[n, 0:192, begin:end])
        results = []
        for tile in tiles:
            at = tile * WIDTH
            z = [product[:, at - begin + k * PTS : at - begin + (k + 1) * PTS] for k in range(CH)]
            coef = coefficients(xs[n, tile])
            hidden = jnp.tanh(z[0] + wide[n, 6])
            squared = hidden * hidden
            one = 1.0 - squared
            two = -2.0 * hidden * one
            three = -2.0 * one * (1.0 - 3.0 * squared)
            mixed = coef[5] * z[5]
            for k in range(1, 5):
                mixed = mixed + coef[k] * z[k]
            curved = coef[5] * (z[1] * z[1] + z[2] * z[2] + z[3] * z[3])
            q = coef[0] * hidden + one * mixed + two * curved
            hi, lo = split2(q)
            qs[n, 0:64, tile * PTS : (tile + 1) * PTS] = hi
            qs[n, 64:128, tile * PTS : (tile + 1) * PTS] = lo
            out = wide[n, 7]
            results.append(jnp.sum(out * q, axis=0, keepdims=True))
            one, two, three = out * one, out * two, out * three
            twice = 2.0 * coef[5] * two
            dlast[n, :, at : at + PTS] = coef[0] * one + two * mixed + three * curved
            for k in range(1, 4):
                dlast[n, :, at + k * PTS : at + (k + 1) * PTS] = coef[k] * one + twice * z[k]
            dlast[n, :, at + 4 * PTS : at + 5 * PTS] = coef[4] * one
            dlast[n, :, at + 5 * PTS : at + 6 * PTS] = coef[5] * one
        return results

    def backward(n, tiles, rows, add):
        begin, end = tiles[0] * WIDTH, (tiles[-1] + 1) * WIDTH

        def collect(ref, value):
            ref[n] = ref[n] + value if add else value

        for tile, row in zip(tiles, rows):
            for k in range(CH):
                at = tile * WIDTH + k * PTS
                put(dz, 0, at, dlast[n, :, at : at + PTS] * row)
        product = dot(lb[n, 1], dz[0, 0:192, begin:end])
        collect(acc3, dot_nt(act2[n, 64:208, begin:end], dz[0, 0:128, begin:end]))
        row = jnp.concatenate(rows, axis=1)
        span = slice(tiles[0] * PTS, (tiles[-1] + 1) * PTS)
        collect(acco, dot_nt(stacked3(row), qs[n, :, span]))
        for tile in tiles:
            at = tile * WIDTH
            a = [product[:, at - begin + k * PTS : at - begin + (k + 1) * PTS] for k in range(CH)]
            z = [state2[n, :, at + k * PTS : at + (k + 1) * PTS] for k in range(CH)]
            squared = z[0] * z[0]
            one = 1.0 - squared
            two = -2.0 * z[0] * one
            three = -2.0 * one * (1.0 - 3.0 * squared)
            mixed = z[5] * a[5]
            for k in range(1, 5):
                mixed = mixed + z[k] * a[k]
            curved = (z[1] * z[1] + z[2] * z[2] + z[3] * z[3]) * a[5]
            put(dz, 1, at, one * a[0] + two * mixed + three * curved)
            twice = 2.0 * two * a[5]
            for k in range(1, 4):
                put(dz, 1, at + k * PTS, one * a[k] + twice * z[k])
            put(dz, 1, at + 4 * PTS, one * a[4])
            put(dz, 1, at + 5 * PTS, one * a[5])
        product = dot(lb[n, 0], dz[1, 0:192, begin:end])
        collect(acc2, dot_nt(act1[n, 64:208, begin:end], dz[1, 0:128, begin:end]))
        total = None
        for tile in tiles:
            at = tile * WIDTH
            a = [product[:, at - begin + k * PTS : at - begin + (k + 1) * PTS] for k in range(CH)]
            hidden = hid1[n, :, tile * PTS : (tile + 1) * PTS]
            squared = hidden * hidden
            one = 1.0 - squared
            two = -2.0 * hidden * one
            three = -2.0 * one * (1.0 - 3.0 * squared)
            mixed = wide[n, 0] * a[1]
            for k in range(1, 4):
                mixed = mixed + wide[n, k] * a[k + 1]
            twice = 2.0 * two * a[5]
            base = tile * WIDTH
            put(dz, 2, base, one * a[0] + two * mixed + three * (wsq[n] * a[5]))
            for k in range(3):
                put(dz, 2, base + (k + 1) * PTS, one * a[k + 1] + twice * wide[n, k])
            put(dz, 2, base + 4 * PTS, one * a[4])
            x = xs[n, tile]
            hi = x.astype(BF).astype(F32)
            top = jnp.where(row8 < 4, hi, jnp.where(row8 == 4, 1.0, 0.0))
            bottom = jnp.where(row8 < 4, x - hi, 0.0)
            pieces = [jnp.concatenate([top, bottom], axis=0)]
            for k in range(4):
                pieces.append(jnp.where(iota((16, PTS), 0) == k, 1.0, 0.0))
            left = jnp.concatenate(pieces, axis=1).astype(BF)
            part = dot_nt(left, dz[2, 0:128, base : base + 5 * PTS])
            total = part if total is None else total + part
        collect(acc1, total)

    def own_forward(n, carry):
        eown[n] = jnp.broadcast_to(forward(n, (0,))[0], (8, PTS))
        return carry

    lax.fori_loop(0, NETS, own_forward, 0)

    arrive(*g_args)
    def choose(parts):
        picked = parts[-1]
        for k in range(len(parts) - 2, -1, -1):
            picked = jnp.where(group == k, parts[k], picked)
        return picked

    blank = jnp.zeros((8, PTS), F32)
    for n in range(NETS):
        b, c = n // 2, n % 2
        slots = [
            gin[0, n],
            gin[1, n],
            gbuf[0, n + 2] if b == 0 else gin[2, n - 2],
            gbuf[0, n - 2] if b == 1 else gin[3, n + 2],
        ]
        xs[n, 1] = choose(slots)
        slots = [
            gbuf[1, n + 1] if c == 0 else gin[4, n - 1],
            gbuf[1, n - 1] if c == 1 else gin[5, n + 1],
            blank,
        ]
        xs[n, 2] = choose(slots)

    def face_forward(n, carry):
        first, second = forward(n, (1, 2))
        ebuf[0, pl.ds(n, 1), :] = first
        ebuf[1, pl.ds(n, 1), :] = second
        return carry

    ebuf[...] = jnp.zeros_like(ebuf)
    lax.fori_loop(0, NETS, face_forward, 0)
    e_args = (lambda slot: ebuf.at[slot // 4], ein, e_send, e_recv, True)
    exchange(*e_args)

    scales = (2.0 / sizes[0], 2.0 / (2 * sizes[1]), 2.0 / (2 * sizes[2]))
    ci = inner[...]
    co = outer[...]
    squares = (
        ci[0:1] * ci[0:1] * (scales[0] * scales[0])
        + ci[1:2] * ci[1:2] * (scales[1] * scales[1])
        + ci[2:3] * ci[2:3] * (scales[2] * scales[2])
    )
    pad = jnp.zeros((3, COARSE), F32)
    c8 = jnp.concatenate([ci, pad], axis=0)
    hi = c8.astype(BF).astype(F32)
    mid = (c8 - hi).astype(BF).astype(F32)
    lo = c8 - hi - mid
    fronts = jnp.concatenate([hi, hi, mid, hi, lo, mid], axis=0).T.astype(BF)
    two_rows = jnp.concatenate(
        [2.0 * co * ci[3:4], 2.0 * co * squares, jnp.zeros((6, COARSE), F32)], axis=0
    ).T
    ccols[0] = jnp.broadcast_to(two_rows[:, 0:1], (COARSE, PTS))
    ccols[1] = jnp.broadcast_to(two_rows[:, 1:2], (COARSE, PTS))
    for j in range(NETS):
        b, c = j // 2, j % 2
        centres = (
            place[0].astype(F32) + 0.5,
            (2 * place[1] + b).astype(F32) + 0.5,
            (2 * place[2] + c).astype(F32) + 0.5,
        )
        own = xs[j, 0]
        v = jnp.where(row8 == 3, own, 0.0)
        for k in range(3):
            v = jnp.where(row8 == k, (centres[k] + own) * scales[k] - 1.0, v)
        v = jnp.where(row8 == 4, 1.0, v)
        cvec[j] = v
        hi = v.astype(BF).astype(F32)
        mid = (v - hi).astype(BF).astype(F32)
        lo = v - hi - mid
        backs = jnp.concatenate([hi, mid, hi, lo, hi, mid], axis=0).astype(BF)
        hidden = jnp.tanh(dot(fronts, backs))
        squared = hidden * hidden
        one = 1.0 - squared
        curve = one * hidden
        bend = one * (1.0 - 3.0 * squared)
        ecoarse[j : j + 1, :] = jnp.sum(
            ccols[0] * one + ccols[1] * (curve * kappa[b, c]), axis=0, keepdims=True
        )
        for k, value in enumerate((curve, bend, one)):
            hi, lo = split2(value)
            cact[2 * k, :, j * PTS : (j + 1) * PTS] = hi
            cact[2 * k + 1, :, j * PTS : (j + 1) * PTS] = lo

    arrive(*e_args)
    for j in range(NETS):
        b, c = j // 2, j % 2

        def row(ref, k):
            return ref[k : k + 1, :]

        first = choose(
            [
                row(ein.at[0], j),
                row(ein.at[1], j),
                row(ebuf.at[0], j - 2) if b == 1 else row(ein.at[2], j + 2),
                row(ebuf.at[0], j + 2) if b == 0 else row(ein.at[3], j - 2),
            ]
        )
        second = choose(
            [
                row(ebuf.at[1], j - 1) if c == 1 else row(ein.at[4], j + 1),
                row(ebuf.at[1], j + 1) if c == 0 else row(ein.at[5], j - 1),
                jnp.zeros((1, PTS), F32),
            ]
        )
        spread = dot_nt(stacked3(jnp.concatenate([first, second], axis=1)), hot[j])
        fine = eown[j, 0:1, :] + spread[0:1] + spread[1:2] + spread[2:3]
        residual = fine + ecoarse[j : j + 1, :] - source[j : j + 1, :]
        res_out[j : j + 1, :] = residual
        scaled = residual * (1.0 / PTS)
        eown[j] = jnp.broadcast_to(scaled, (8, PTS))
        moved = dot(stacked3(scaled), hot[j])
        moved = moved[0:1] + moved[1:2] + moved[2:3]
        rbuf[0, j : j + 1, :] = moved[:, 0:PTS]
        rbuf[1, j : j + 1, :] = moved[:, PTS : 2 * PTS]
    rbuf[:, 4:8, :] = jnp.zeros((2, 4, PTS), F32)
    r_args = (lambda slot: rbuf.at[slot // 4], rin, r_send, r_recv, False)
    exchange(*r_args)

    blocks = []
    for j in range(NETS):
        b, c = j // 2, j % 2
        plain = eown[j] * cvec[j]
        plain = jnp.concatenate([plain, plain * kappa[b, c]], axis=0)
        hi = plain.astype(BF).astype(F32)
        blocks.append(jnp.concatenate([hi, plain - hi], axis=0))
    left = jnp.concatenate(blocks, axis=1).astype(BF)
    sums = []
    for k in range(3):
        upper = dot_nt(left, cact[2 * k])
        lower = dot_nt(left, cact[2 * k + 1])
        sums.append(upper[0:16] + upper[16:32] + lower[0:16])
    s_one, s_curve = sums[2][4:5], sums[0][12:13]
    moments = co * (2.0 * squares * sums[1][8:13] - 4.0 * ci[3:4] * sums[0][0:5])
    extra = jnp.concatenate(
        [
            (4.0 * scales[0] * scales[0]) * ci[0:1] * co * s_curve,
            (4.0 * scales[1] * scales[1]) * ci[1:2] * co * s_curve,
            (4.0 * scales[2] * scales[2]) * ci[2:3] * co * s_curve,
            2.0 * co * s_one,
            jnp.zeros((1, COARSE), F32),
        ],
        axis=0,
    )
    outer_grad = 2.0 * ci[3:4] * s_one + 2.0 * squares * s_curve
    partial_sums = jnp.concatenate(
        [moments + extra, outer_grad, jnp.zeros((2, COARSE), F32)], axis=0
    )
    ar_start(0, partial_sums)

    def own_backward(n, carry):
        backward(n, (0,), [eown[n, 0:1, :]], False)
        return carry

    lax.fori_loop(0, 2, own_backward, 0)
    ar_start(1, ar_finish(0))
    lax.fori_loop(2, NETS, own_backward, 0)
    ar_start(2, ar_finish(1))

    arrive(*r_args)
    for n in range(NETS):
        b, c = n // 2, n % 2
        first = choose(
            [
                rin[0, n : n + 1, :],
                rin[1, n : n + 1, :],
                rbuf[0, n + 2 : n + 3, :] if b == 0 else rin[2, n - 2 : n - 1, :],
                rbuf[0, n - 2 : n - 1, :] if b == 1 else rin[3, n + 2 : n + 3, :],
            ]
        )
        second = choose(
            [
                rbuf[1, n + 1 : n + 2, :] if c == 0 else rin[4, n - 1 : n, :],
                rbuf[1, n - 1 : n, :] if c == 1 else rin[5, n + 1 : n + 2, :],
                jnp.zeros((1, PTS), F32),
            ]
        )
        cols[n, 0] = jnp.broadcast_to(first, (8, PTS))
        cols[n, 1] = jnp.broadcast_to(second, (8, PTS))

    def face_backward(n, carry):
        backward(n, (1, 2), [cols[n, 0, 0:1, :], cols[n, 1, 0:1, :]], True)
        joined = []
        for ref in (acc2, acc3):
            low_rows = ref[n, 0:64, :]
            high_rows = ref[n, 64:128, :]
            joined.append(low_rows[:, 0:64] + high_rows[:, 0:64] + high_rows[:, 64:128])
        work[...] = jnp.concatenate(joined, axis=1)
        even = work[pl.ds(0, 32, stride=2), :]
        odd = work[pl.ds(1, 32, stride=2), :]
        bias2 = acc2[n, 128:129, :]
        bias3 = acc3[n, 128:129, :]
        bias2 = bias2[:, 0:64] + bias2[:, 64:128]
        bias3 = bias3[:, 0:64] + bias3[:, 64:128]
        first = acc1[n, 0:8, :] + acc1[n, 8:16, :]
        first = first[:, 0:64] + first[:, 64:128]
        last = acco[n, 0:1, :] + acco[n, 1:2, :] + acco[n, 2:3, :]
        last = last[:, 0:64] + last[:, 64:128]
        grad_out[n, 0:1, 0:64] = first[0:1]
        grad_out[n, 0:1, 64:128] = first[1:2]
        grad_out[n, 1:2, 0:64] = first[2:3]
        grad_out[n, 1:2, 64:128] = first[3:4]
        grad_out[n, 2:3, 0:64] = first[4:5]
        grad_out[n, 2:34, 64:128] = even[:, 0:64]
        grad_out[n, 3:35, 0:64] = odd[:, 0:64]
        grad_out[n, 34:35, 64:128] = bias2
        grad_out[n, 35:67, 0:64] = even[:, 64:128]
        grad_out[n, 35:67, 64:128] = odd[:, 64:128]
        grad_out[n, 67:68, 0:64] = bias3
        grad_out[n, 67:68, 64:128] = last
        return carry

    lax.fori_loop(0, 2, face_backward, 0)
    ar_start(3, ar_finish(2))
    lax.fori_loop(2, NETS, face_backward, 0)
    count = NETS * sizes[0] * sizes[1] * sizes[2]
    coarse_out[...] = ar_finish(3) * (count ** (-0.5))

    for args in (g_args, e_args, r_args):
        sent(*args)
    for stage in range(4):
        for out in ar_copies(stage, False):
            out.wait_send()


def on_device(fine_params, coarse_inner, coarse_outer, points, source, conductivity, face_points):
    sizes = tuple(lax.axis_size(axis) for axis in AXES)
    vmem = pl.BlockSpec(memory_space=pltpu.VMEM)
    smem = pl.BlockSpec(memory_space=pltpu.SMEM)
    residual, grads, coarse = pl.pallas_call(
        partial(kernel, sizes),
        out_shape=(
            jax.ShapeDtypeStruct((NETS, PTS), F32),
            jax.ShapeDtypeStruct((NETS, ROWS, PTS), F32),
            jax.ShapeDtypeStruct((8, COARSE), F32),
        ),
        in_specs=[vmem, vmem, vmem, vmem, vmem, smem, vmem],
        out_specs=(vmem, vmem, vmem),
        scratch_shapes=[
            pltpu.VMEM((NETS, PTS, 2 * PTS), BF),
            pltpu.VMEM((2, NETS, 8, PTS), F32),
            pltpu.VMEM((6, NETS, 8, PTS), F32),
            pltpu.VMEM((2, 8, PTS), F32),
            pltpu.VMEM((6, 8, PTS), F32),
            pltpu.VMEM((2, 8, PTS), F32),
            pltpu.VMEM((6, 8, PTS), F32),
            pltpu.VMEM((NETS, 3, 8, PTS), F32),
            pltpu.VMEM((NETS, 2, 8, PTS), F32),
            pltpu.VMEM((NETS, 8, HID, PTS), F32),
            pltpu.VMEM((NETS, HID, PTS), F32),
            pltpu.VMEM((NETS, 2, HID, 3 * HID), BF),
            pltpu.VMEM((NETS, 2, HID, 3 * HID), BF),
            pltpu.VMEM((NETS, 208, 3 * WIDTH), BF),
            pltpu.VMEM((NETS, 208, 3 * WIDTH), BF),
            pltpu.VMEM((NETS, HID, 3 * PTS), F32),
            pltpu.VMEM((NETS, HID, 3 * WIDTH), F32),
            pltpu.VMEM((NETS, HID, 3 * WIDTH), F32),
            pltpu.VMEM((NETS, PTS, 3 * PTS), BF),
            pltpu.VMEM((3, 192, 3 * WIDTH), BF),
            pltpu.VMEM((NETS, 144, PTS), F32),
            pltpu.VMEM((NETS, 144, PTS), F32),
            pltpu.VMEM((NETS, 16, PTS), F32),
            pltpu.VMEM((NETS, 16, PTS), F32),
            pltpu.VMEM((HID, PTS), F32),
            pltpu.VMEM((NETS, 8, PTS), F32),
            pltpu.VMEM((8, PTS), F32),
            pltpu.VMEM((2, COARSE, PTS), F32),
            pltpu.VMEM((6, COARSE, NETS * PTS), BF),
            pltpu.VMEM((NETS, 8, PTS), F32),
            pltpu.VMEM((4, 4, 8, COARSE), F32),
            pltpu.SemaphoreType.DMA((6,)),
            pltpu.SemaphoreType.DMA((6,)),
            pltpu.SemaphoreType.DMA((6,)),
            pltpu.SemaphoreType.DMA((6,)),
            pltpu.SemaphoreType.DMA((6,)),
            pltpu.SemaphoreType.DMA((6,)),
            pltpu.SemaphoreType.DMA((4, 4)),
            pltpu.SemaphoreType.DMA((4, 4)),
        ],
        compiler_params=pltpu.CompilerParams(
            collective_id=0, has_side_effects=True, vmem_limit_bytes=48 * 1024 * 1024
        ),
    )(
        fine_params.reshape(NETS, ROWS, PTS),
        coarse_inner,
        coarse_outer.reshape(1, COARSE),
        points.reshape(NETS, 4, PTS),
        source.reshape(NETS, PTS),
        conductivity.reshape(2, 2),
        face_points.reshape(NETS, 6, FACE),
    )
    return (
        residual.reshape(source.shape),
        grads.reshape(fine_params.shape),
        coarse[0:5],
        coarse[5],
    )


def solution(mesh):
    return jax.shard_map(
        on_device,
        mesh=mesh,
        in_specs=(
            P("gx", "gy", "gz", None),
            P(),
            P(),
            P("gx", "gy", "gz", None, None),
            P("gx", "gy", "gz", None),
            P("gx", "gy", "gz"),
            P("gx", "gy", "gz", None, None),
        ),
        out_specs=(P("gx", "gy", "gz", None), P("gx", "gy", "gz", None), P(), P()),
        check_vma=False,
    )
```

```python
from functools import partial

import jax
import jax.numpy as jnp
from jax import lax
from jax.experimental import pallas as pl
from jax.experimental.pallas import tpu as pltpu
from jax.sharding import PartitionSpec as P

PTS = 128
FACE = 32
HID = 64
COARSE = 512
ROWS = 68
NETS = 4
CH = 6
WIDTH = CH * PTS
AXES = ("gx", "gy", "gz")
MESH = pl.DeviceIdType.MESH
BF = jnp.bfloat16
F32 = jnp.float32


def split2(x):
    hi = x.astype(BF)
    return hi, (x - hi.astype(F32)).astype(BF)


def split3(x):
    hi = x.astype(BF)
    rest = x - hi.astype(F32)
    mid = rest.astype(BF)
    return hi, mid, (rest - mid.astype(F32)).astype(BF)


def dot(a, b):
    return lax.dot_general(a, b, (((1,), (0,)), ((), ())), preferred_element_type=F32)


def dot_nt(a, b):
    return lax.dot_general(a, b, (((1,), (1,)), ((), ())), preferred_element_type=F32)


def iota(shape, dim):
    return lax.broadcasted_iota(jnp.int32, shape, dim)


def stacked3(row):
    which = iota((16, row.shape[1]), 0)
    hi = row.astype(BF).astype(F32)
    rest = row - hi
    mid = rest.astype(BF).astype(F32)
    low = rest - mid
    rows = jnp.where(which == 0, hi, jnp.where(which == 1, mid, jnp.where(which == 2, low, 0.0)))
    return rows.astype(BF)


def coefficients(x):
    sx, sy, sz, kappa = x[0:1], x[1:2], x[2:3], x[4:5]
    square = sx * sx + sy * sy + sz * sz
    window = jnp.exp(-square)
    scaled = kappa * window
    return (
        scaled * (6.0 - 4.0 * square),
        4.0 * scaled * sx,
        4.0 * scaled * sy,
        4.0 * scaled * sz,
        2.0 * window,
        -scaled,
    )


def kernel(
    sizes,
    params_hbm,
    inner_hbm,
    outer_hbm,
    points_hbm,
    source_hbm,
    kappa_hbm,
    faces_hbm,
    res_far,
    grad_far,
    inner_far,
    outer_far,
    res_out,
    grad_out,
    inner_out,
    outer_out,
    out_sem,
    params,
    inner,
    outer,
    points,
    source,
    kappa,
    faces,
    in_sem,
    hot,
    gbuf,
    gin,
    ebuf,
    ein,
    rbuf,
    rin,
    xs,
    cols,
    wide,
    wsq,
    lf,
    lb,
    act1,
    act2,
    hid1,
    state2,
    state3,
    qs,
    dz,
    acc3,
    acc2,
    acc1,
    acco,
    work,
    eown,
    ccols,
    cact,
    cone,
    csums,
    ar,
    g_send,
    g_recv,
    e_send,
    e_recv,
    r_send,
    r_recv,
    ar_send,
    ar_recv,
    tokens,
    flat_out,
):
    place = [lax.axis_index(axis) for axis in AXES]
    fetches = [
        pltpu.make_async_copy(far, near, in_sem.at[k])
        for k, (far, near) in enumerate(
            (
                (points_hbm, points),
                (faces_hbm, faces),
                (kappa_hbm, kappa),
                (params_hbm, params),
                (inner_hbm, inner),
                (outer_hbm, outer),
                (source_hbm, source),
            )
        )
    ]
    for fetch in fetches:
        fetch.start()

    def target(slot, flip):
        axis = slot // 2
        sign = (2 * (slot % 2) - 1) * (-1 if flip else 1)
        return AXES[axis], place[axis] + sign, sizes[axis]

    groups = [
        (
            place[1] * sizes[2] + place[2],
            sizes[1] * sizes[2],
            lambda p: {"gy": p // sizes[2], "gz": lax.rem(p, sizes[2])},
        ),
        (place[0], sizes[0], lambda p: {"gx": p}),
    ]

    def ring(axis, step):
        return {AXES[axis]: lax.rem(place[axis] + step + sizes[axis], sizes[axis])}

    def pass_on(level, axes):
        for axis in axes:
            reach = (1 << level) if axis == 0 else 1
            for side in range(2):
                pl.semaphore_signal(
                    tokens.at[level, 2 * axis + side],
                    inc=1,
                    device_id=ring(axis, reach if side else -reach),
                    device_id_type=MESH,
                )

    def hear(level, axes):
        for axis in axes:
            for side in range(2):
                pl.semaphore_wait(tokens.at[level, 2 * axis + side], 1)

    def exchange(source_of, landing, send_sem, recv_sem, flip):
        for slot in range(6):
            axis, where, size = target(slot, flip)

            @pl.when(jnp.logical_and(where >= 0, where < size))
            def _(slot=slot, axis=axis, where=where):
                pltpu.make_async_remote_copy(
                    source_of(slot), landing.at[slot], send_sem.at[slot], recv_sem.at[slot],
                    device_id={axis: where}, device_id_type=MESH,
                ).start()

    def arrive(source_of, landing, send_sem, recv_sem, flip):
        for slot in range(6):
            axis, where, size = target(slot, not flip)

            @pl.when(jnp.logical_and(where >= 0, where < size))
            def _(slot=slot, axis=axis, where=where):
                pltpu.make_async_remote_copy(
                    source_of(slot), landing.at[slot], send_sem.at[slot], recv_sem.at[slot],
                    device_id={axis: where}, device_id_type=MESH,
                ).wait_recv()

    def sent(source_of, landing, send_sem, recv_sem, flip):
        for slot in range(6):
            axis, where, size = target(slot, flip)

            @pl.when(jnp.logical_and(where >= 0, where < size))
            def _(slot=slot, axis=axis, where=where):
                pltpu.make_async_remote_copy(
                    source_of(slot), landing.at[slot], send_sem.at[slot], recv_sem.at[slot],
                    device_id={axis: where}, device_id_type=MESH,
                ).wait_send()

    def ar_copies(stage, arriving):
        pos, size, member = groups[stage]
        for k in range(1, size):
            partner = lax.rem(pos + k, size)
            slot = partner if arriving else pos
            yield pltpu.make_async_remote_copy(
                ar.at[stage, pos], ar.at[stage, slot],
                ar_send.at[stage, partner], ar_recv.at[stage, slot],
                device_id=member(partner), device_id_type=MESH,
            )

    def ar_start(stage, value):
        ar[stage, groups[stage][0]] = value
        for out in ar_copies(stage, False):
            out.start()

    def ar_finish(stage):
        for back in ar_copies(stage, True):
            back.wait_recv()
        total = ar[stage, 0]
        for p in range(1, groups[stage][1]):
            total = total + ar[stage, p]
        return total

    gin[...] = jnp.zeros_like(gin)
    ein[...] = jnp.zeros_like(ein)
    rin[...] = jnp.zeros_like(rin)

    barrier = pltpu.get_barrier_semaphore()
    for axis in range(3):
        for step in (-1, 1):
            pl.semaphore_signal(barrier, inc=1, device_id=ring(axis, step), device_id_type=MESH)

    lane = iota((1, PTS), 1)
    row8 = iota((8, PTS), 0)
    group = lane // FACE
    for fetch in fetches[0:3]:
        fetch.wait()
    for j in range(NETS):
        b, c = j // 2, j % 2
        index = [faces[b, k, c : c + 1, :] for k in range(6)]
        first = jnp.concatenate(index[0:4], axis=1)
        second = jnp.concatenate(index[4:6] + [jnp.full((1, 2 * FACE), -1, jnp.int32)], axis=1)
        point = iota((PTS, PTS), 0)
        hot[j, :, 0:PTS] = jnp.where(point == first, 1.0, 0.0).astype(BF)
        hot[j, :, PTS : 2 * PTS] = jnp.where(point == second, 1.0, 0.0).astype(BF)
        own = jnp.concatenate([points[j], jnp.zeros((4, PTS), F32)], axis=0)
        own = jnp.where(row8 == 4, kappa[b : b + 1, c : c + 1], own)
        own = jnp.where(row8 == 5, 1.0, own)
        xs[j, 0] = own
        hi, mid, low_part = split3(own)
        pieces = jnp.concatenate([hi, mid, low_part, jnp.zeros_like(hi)], axis=0)
        moved = dot(pieces, hot[j])
        moved = moved[0:8] + moved[8:16] + moved[16:24]
        shift_a = jnp.where(row8 == group // 2, (2 * (group % 2) - 1).astype(F32), 0.0)
        shift_b = jnp.where(row8 == 2, jnp.where(group < 2, (2 * (group % 2) - 1).astype(F32), 0.0), 0.0)
        gbuf[0, j] = moved[:, 0:PTS] - shift_a
        gbuf[1, j] = moved[:, PTS : 2 * PTS] - shift_b

    pl.semaphore_wait(barrier, 6)
    g_args = (lambda slot: gbuf.at[slot // 4], gin, g_send, g_recv, False)
    exchange(*g_args)
    pass_on(0, (0, 1, 2))

    for fetch in fetches[3:]:
        fetch.wait()
    half = iota((32, PTS), 1) < HID
    for n in range(NETS):
        flat = params[n // 2, :, n % 2, :]
        even = pltpu.roll(jnp.where(half, flat[35:67], flat[2:34]), HID, 1)
        odd = jnp.where(half, flat[3:35], flat[35:67])
        work[pl.ds(0, 32, stride=2), :] = even
        work[pl.ds(1, 32, stride=2), :] = odd
        both = work[...]
        hi, lo = split2(both)
        lb[n, 0, :, 0:64] = hi[:, 0:64]
        lb[n, 0, :, 64:128] = hi[:, 0:64]
        lb[n, 0, :, 128:192] = lo[:, 0:64]
        lb[n, 1, :, 0:64] = hi[:, 64:128]
        lb[n, 1, :, 64:128] = hi[:, 64:128]
        lb[n, 1, :, 128:192] = lo[:, 64:128]
        hi, lo = split2(both.T)
        for layer in range(2):
            lf[n, layer, :, 0:64] = hi[64 * layer : 64 * layer + 64]
            lf[n, layer, :, 64:128] = hi[64 * layer : 64 * layer + 64]
            lf[n, layer, :, 128:192] = lo[64 * layer : 64 * layer + 64]
        vectors = jnp.concatenate(
            [
                flat[0:1],
                pltpu.roll(flat[0:1], HID, 1),
                flat[1:2],
                pltpu.roll(flat[1:2], HID, 1),
                flat[2:3],
                pltpu.roll(flat[34:35], HID, 1),
                flat[67:68],
                pltpu.roll(flat[67:68], HID, 1),
            ],
            axis=0,
        )
        columns = vectors.T
        for k in range(8):
            wide[n, k] = jnp.broadcast_to(columns[0:64, k : k + 1], (64, PTS))
        wsq[n] = wide[n, 0] * wide[n, 0] + wide[n, 1] * wide[n, 1] + wide[n, 2] * wide[n, 2]
        first_channel = jnp.where(
            jnp.logical_and(iota((16, PTS), 0) == 0, iota((16, PTS), 1) >= 0), 1.0, 0.0
        ).astype(BF)
        for tile in range(3):
            for k in range(CH):
                at = (tile * CH + k) * PTS
                value = first_channel if k == 0 else jnp.zeros_like(first_channel)
                act1[n, 192:208, at : at + PTS] = value
                act2[n, 192:208, at : at + PTS] = value

    def put(ref, n, at, value):
        hi, lo = split2(value)
        ref[n, 0:64, at : at + PTS] = hi
        ref[n, 64:128, at : at + PTS] = lo
        ref[n, 128:192, at : at + PTS] = hi

    def forward(n, tiles):
        begin, end = tiles[0] * WIDTH, (tiles[-1] + 1) * WIDTH
        for tile in tiles:
            x = xs[n, tile]
            pre = (
                wide[n, 4]
                + wide[n, 0] * x[0:1]
                + wide[n, 1] * x[1:2]
                + wide[n, 2] * x[2:3]
                + wide[n, 3] * x[3:4]
            )
            hidden = jnp.tanh(pre)
            one = 1.0 - hidden * hidden
            two = -2.0 * hidden * one
            hid1[n, :, tile * PTS : (tile + 1) * PTS] = hidden
            at = tile * WIDTH
            put(act1, n, at, hidden)
            for k in range(4):
                put(act1, n, at + (k + 1) * PTS, one * wide[n, k])
            put(act1, n, at + 5 * PTS, two * wsq[n])
        product = dot(lf[n, 0], act1[n, 0:192, begin:end])
        for tile in tiles:
            at = tile * WIDTH
            z = [product[:, at - begin + k * PTS : at - begin + (k + 1) * PTS] for k in range(CH)]
            hidden = jnp.tanh(z[0] + wide[n, 5])
            one = 1.0 - hidden * hidden
            two = -2.0 * hidden * one
            state2[n, :, at : at + PTS] = hidden
            for k in range(1, CH):
                state2[n, :, at + k * PTS : at + (k + 1) * PTS] = z[k]
            put(act2, n, at, hidden)
            for k in range(1, 5):
                put(act2, n, at + k * PTS, one * z[k])
            put(act2, n, at + 5 * PTS, two * (z[1] * z[1] + z[2] * z[2] + z[3] * z[3]) + one * z[5])
        product = dot(lf[n, 1], act2[n, 0:192, begin:end])
        results = []
        for tile in tiles:
            at = tile * WIDTH
            z = [product[:, at - begin + k * PTS : at - begin + (k + 1) * PTS] for k in range(CH)]
            coef = coefficients(xs[n, tile])
            hidden = jnp.tanh(z[0] + wide[n, 6])
            one = 1.0 - hidden * hidden
            two = -2.0 * hidden * one
            mixed = coef[5] * z[5]
            for k in range(1, 5):
                mixed = mixed + coef[k] * z[k]
            curved = coef[5] * (z[1] * z[1] + z[2] * z[2] + z[3] * z[3])
            q = coef[0] * hidden + one * mixed + two * curved
            state3[n, :, at : at + PTS] = hidden
            for k in range(1, 4):
                state3[n, :, at + k * PTS : at + (k + 1) * PTS] = z[k]
            state3[n, :, at + 4 * PTS : at + 5 * PTS] = mixed
            state3[n, :, at + 5 * PTS : at + 6 * PTS] = q
            results.append(jnp.sum(wide[n, 7] * q, axis=0, keepdims=True))
        return results

    def backward(n, tiles, rows, add):
        begin, end = tiles[0] * WIDTH, (tiles[-1] + 1) * WIDTH

        def collect(ref, value):
            ref[n] = ref[n] + value if add else value

        for tile, row in zip(tiles, rows):
            at = tile * WIDTH
            coef = [value * row for value in coefficients(xs[n, tile])]
            hidden, z1, z2, z3, mixed, q = (
                state3[n, :, at + k * PTS : at + (k + 1) * PTS] for k in range(CH)
            )
            hi, lo = split2(q)
            qs[n, 0:64, tile * PTS : (tile + 1) * PTS] = hi
            qs[n, 64:128, tile * PTS : (tile + 1) * PTS] = lo
            squared = hidden * hidden
            one = 1.0 - squared
            three = -2.0 * one * (1.0 - 3.0 * squared)
            out = wide[n, 7]
            one = out * one
            two = -2.0 * hidden * one
            curved = coef[5] * (z1 * z1 + z2 * z2 + z3 * z3)
            put(dz, 0, at, coef[0] * one + two * (mixed * row) + (out * three) * curved)
            twice = 2.0 * coef[5] * two
            for k, z in ((1, z1), (2, z2), (3, z3)):
                put(dz, 0, at + k * PTS, coef[k] * one + twice * z)
            put(dz, 0, at + 4 * PTS, coef[4] * one)
            put(dz, 0, at + 5 * PTS, coef[5] * one)
        product = dot(lb[n, 1], dz[0, 0:192, begin:end])
        collect(acc3, dot_nt(act2[n, 64:208, begin:end], dz[0, 0:128, begin:end]))
        row = jnp.concatenate(rows, axis=1)
        span = slice(tiles[0] * PTS, (tiles[-1] + 1) * PTS)
        collect(acco, dot_nt(stacked3(row), qs[n, :, span]))
        for tile in tiles:
            at = tile * WIDTH
            a = [product[:, at - begin + k * PTS : at - begin + (k + 1) * PTS] for k in range(CH)]
            z = [state2[n, :, at + k * PTS : at + (k + 1) * PTS] for k in range(CH)]
            squared = z[0] * z[0]
            one = 1.0 - squared
            two = -2.0 * z[0] * one
            three = -2.0 * one * (1.0 - 3.0 * squared)
            mixed = z[5] * a[5]
            for k in range(1, 5):
                mixed = mixed + z[k] * a[k]
            curved = (z[1] * z[1] + z[2] * z[2] + z[3] * z[3]) * a[5]
            put(dz, 1, at, one * a[0] + two * mixed + three * curved)
            twice = 2.0 * two * a[5]
            for k in range(1, 4):
                put(dz, 1, at + k * PTS, one * a[k] + twice * z[k])
            put(dz, 1, at + 4 * PTS, one * a[4])
            put(dz, 1, at + 5 * PTS, one * a[5])
        product = dot(lb[n, 0], dz[1, 0:192, begin:end])
        collect(acc2, dot_nt(act1[n, 64:208, begin:end], dz[1, 0:128, begin:end]))
        total = None
        for tile in tiles:
            at = tile * WIDTH
            a = [product[:, at - begin + k * PTS : at - begin + (k + 1) * PTS] for k in range(CH)]
            hidden = hid1[n, :, tile * PTS : (tile + 1) * PTS]
            squared = hidden * hidden
            one = 1.0 - squared
            two = -2.0 * hidden * one
            three = -2.0 * one * (1.0 - 3.0 * squared)
            mixed = wide[n, 0] * a[1]
            for k in range(1, 4):
                mixed = mixed + wide[n, k] * a[k + 1]
            twice = 2.0 * two * a[5]
            base = tile * WIDTH
            put(dz, 2, base, one * a[0] + two * mixed + three * (wsq[n] * a[5]))
            for k in range(3):
                put(dz, 2, base + (k + 1) * PTS, one * a[k + 1] + twice * wide[n, k])
            put(dz, 2, base + 4 * PTS, one * a[4])
            x = xs[n, tile]
            hi = x.astype(BF).astype(F32)
            top = jnp.where(row8 < 4, hi, jnp.where(row8 == 4, 1.0, 0.0))
            bottom = jnp.where(row8 < 4, x - hi, 0.0)
            pieces = [jnp.concatenate([top, bottom], axis=0)]
            for k in range(4):
                pieces.append(jnp.where(iota((16, PTS), 0) == k, 1.0, 0.0))
            left = jnp.concatenate(pieces, axis=1).astype(BF)
            part = dot_nt(left, dz[2, 0:128, base : base + 5 * PTS])
            total = part if total is None else total + part
        collect(acc1, total)

    def own_forward(n, carry):
        eown[n] = jnp.broadcast_to(forward(n, (0,))[0], (8, PTS))
        return carry

    lax.fori_loop(0, NETS, own_forward, 0)

    scales = (2.0 / sizes[0], 2.0 / (2 * sizes[1]), 2.0 / (2 * sizes[2]))
    ci = inner[...]
    co = outer[...]
    squares = (
        ci[0:1] * ci[0:1] * (scales[0] * scales[0])
        + ci[1:2] * ci[1:2] * (scales[1] * scales[1])
        + ci[2:3] * ci[2:3] * (scales[2] * scales[2])
    )
    pad = jnp.zeros((3, COARSE), F32)
    c8 = jnp.concatenate([ci, pad], axis=0)
    hi = c8.astype(BF).astype(F32)
    mid = (c8 - hi).astype(BF).astype(F32)
    lo = c8 - hi - mid
    fronts = jnp.concatenate([hi, hi, mid, hi, lo, mid], axis=0).T.astype(BF)
    two_rows = jnp.concatenate(
        [2.0 * co * ci[3:4], 2.0 * co * squares, jnp.zeros((6, COARSE), F32)], axis=0
    ).T
    ccols[0] = jnp.broadcast_to(two_rows[:, 0:1], (COARSE, PTS))
    ccols[1] = jnp.broadcast_to(two_rows[:, 1:2], (COARSE, PTS))

    def coarse_inputs(n, x):
        b, c = n // 2, n % 2
        centres = (
            place[0].astype(F32) + 0.5,
            (2 * place[1] + b).astype(F32) + 0.5,
            (2 * place[2] + c).astype(F32) + 0.5,
        )
        v = jnp.where(row8 == 3, x, 0.0)
        for k in range(3):
            v = jnp.where(row8 == k, (centres[k] + x) * scales[k] - 1.0, v)
        return jnp.where(row8 == 4, 1.0, v)

    def coarse_forward(block, v, wanted):
        hi = v.astype(BF).astype(F32)
        mid = (v - hi).astype(BF).astype(F32)
        lo = v - hi - mid
        backs = jnp.concatenate([hi, mid, hi, lo, hi, mid], axis=0).astype(BF)
        hidden = jnp.tanh(dot(fronts, backs))
        squared = hidden * hidden
        one = 1.0 - squared
        curve = one * hidden
        bend = one * (1.0 - 3.0 * squared)
        cone[:, block * PTS : (block + 1) * PTS] = one
        for k, value in enumerate((curve, bend)):
            hi, lo = split2(value)
            cact[2 * k, :, block * PTS : (block + 1) * PTS] = hi
            cact[2 * k + 1, :, block * PTS : (block + 1) * PTS] = lo
        if wanted is not None:
            return jnp.sum(
                ccols[0] * one + ccols[1] * (curve * wanted), axis=0, keepdims=True
            )

    def coarse_sums(blocks, first):
        lefts = []
        for weight, v, conductivity in blocks:
            plain = weight * v
            plain = jnp.concatenate([plain, plain * conductivity], axis=0)
            hi = plain.astype(BF).astype(F32)
            lefts.append(jnp.concatenate([hi, plain - hi], axis=0))
        left = jnp.concatenate(lefts, axis=1).astype(BF)
        span = slice(first * PTS, (first + len(blocks)) * PTS)
        sums = []
        for k in range(2):
            upper = dot_nt(left, cact[2 * k, :, span])
            lower = dot_nt(left, cact[2 * k + 1, :, span])
            sums.append(upper[0:16] + upper[16:32] + lower[0:16])
        weighted = None
        for k, (weight, _, _) in enumerate(blocks):
            term = cone[:, (first + k) * PTS : (first + k + 1) * PTS] * weight
            weighted = term if weighted is None else weighted + term
        hi, lo = split2(weighted)
        ones = jnp.ones((16, PTS), BF)
        sums.append(dot_nt(ones, hi) + dot_nt(ones, lo))
        return sums

    blocks = []
    for j in range(NETS):
        x = xs[j, 0]
        v = coarse_inputs(j, x)
        base = eown[j, 0:1, :] + coarse_forward(j, v, x[4:5]) - source[j : j + 1, :]
        eown[j, 0:1, :] = base
        blocks.append((base * (1.0 / PTS), v, x[4:5]))
    own_sums = coarse_sums(blocks, 0)
    for k in range(3):
        csums[k] = own_sums[k]

    hear(0, (0, 1, 2))
    pass_on(1, (0, 1, 2))

    arrive(*g_args)
    def choose(parts):
        picked = parts[-1]
        for k in range(len(parts) - 2, -1, -1):
            picked = jnp.where(group == k, parts[k], picked)
        return picked

    blank = jnp.zeros((8, PTS), F32)
    for n in range(NETS):
        b, c = n // 2, n % 2
        slots = [
            gin[0, n],
            gin[1, n],
            gbuf[0, n + 2] if b == 0 else gin[2, n - 2],
            gbuf[0, n - 2] if b == 1 else gin[3, n + 2],
        ]
        xs[n, 1] = choose(slots)
        slots = [
            gbuf[1, n + 1] if c == 0 else gin[4, n - 1],
            gbuf[1, n - 1] if c == 1 else gin[5, n + 1],
            blank,
        ]
        xs[n, 2] = choose(slots)

    def face_forward(n, carry):
        first, second = forward(n, (1, 2))
        ebuf[0, pl.ds(n, 1), :] = first
        ebuf[1, pl.ds(n, 1), :] = second
        return carry

    ebuf[...] = jnp.zeros_like(ebuf)
    lax.fori_loop(0, 2, face_forward, 0)
    hear(1, (1, 2))
    pass_on(2, (1, 2))
    lax.fori_loop(2, NETS, face_forward, 0)
    e_args = (lambda slot: ebuf.at[slot // 4], ein, e_send, e_recv, True)
    exchange(*e_args)

    hear(1, (0,))
    pass_on(2, (0,))
    def joined_halves(first, second):
        return jnp.where(lane < HID, first, pltpu.roll(second, HID, 1))

    weights, inputs, levels = [], [], []
    for n in range(NETS):
        for tile in range(2):
            x = xs[n, tile + 1]
            weights.append(ebuf[tile, n : n + 1, :] * x[5:6] * (1.0 / PTS))
            inputs.append(coarse_inputs(n, x))
            levels.append(x[4:5])
    blocks = [(weights[2 * n], inputs[2 * n], levels[2 * n]) for n in range(NETS)]
    for n in range(0, NETS, 2):
        blocks.append(
            tuple(
                joined_halves(values[2 * n + 1], values[2 * n + 3])
                for values in (weights, inputs, levels)
            )
        )
    for k, (_, v, _) in enumerate(blocks):
        coarse_forward(NETS + k, v, None)
    sums = [csums[k] + part for k, part in enumerate(coarse_sums(blocks, NETS))]
    s_one, s_curve = sums[2][0:1], sums[0][12:13]
    moments = co * (2.0 * squares * sums[1][8:13] - 4.0 * ci[3:4] * sums[0][0:5])
    extra = jnp.concatenate(
        [
            (4.0 * scales[0] * scales[0]) * ci[0:1] * co * s_curve,
            (4.0 * scales[1] * scales[1]) * ci[1:2] * co * s_curve,
            (4.0 * scales[2] * scales[2]) * ci[2:3] * co * s_curve,
            2.0 * co * s_one,
            jnp.zeros((1, COARSE), F32),
        ],
        axis=0,
    )
    outer_grad = 2.0 * ci[3:4] * s_one + 2.0 * squares * s_curve
    partial_sums = jnp.concatenate([moments + extra, outer_grad], axis=0)
    hear(2, (1, 2))
    ar_start(
        0,
        jnp.concatenate([partial_sums[:, k * PTS : (k + 1) * PTS] for k in range(4)], axis=0),
    )

    arrive(*e_args)
    for j in range(NETS):
        b, c = j // 2, j % 2

        def row(ref, k):
            return ref[k : k + 1, :]

        first = choose(
            [
                row(ein.at[0], j),
                row(ein.at[1], j),
                row(ebuf.at[0], j - 2) if b == 1 else row(ein.at[2], j + 2),
                row(ebuf.at[0], j + 2) if b == 0 else row(ein.at[3], j - 2),
            ]
        )
        second = choose(
            [
                row(ebuf.at[1], j - 1) if c == 1 else row(ein.at[4], j + 1),
                row(ebuf.at[1], j + 1) if c == 0 else row(ein.at[5], j - 1),
                jnp.zeros((1, PTS), F32),
            ]
        )
        spread = dot_nt(stacked3(jnp.concatenate([first, second], axis=1)), hot[j])
        residual = eown[j, 0:1, :] + spread[0:1] + spread[1:2] + spread[2:3]
        res_out[j : j + 1, :] = residual
        scaled = residual * (1.0 / PTS)
        eown[j] = jnp.broadcast_to(scaled, (8, PTS))
        moved = dot(stacked3(scaled), hot[j])
        moved = moved[0:1] + moved[1:2] + moved[2:3]
        rbuf[0, j : j + 1, :] = moved[:, 0:PTS]
        rbuf[1, j : j + 1, :] = moved[:, PTS : 2 * PTS]
    rbuf[:, 4:8, :] = jnp.zeros((2, 4, PTS), F32)
    r_args = (lambda slot: rbuf.at[slot // 4], rin, r_send, r_recv, False)
    exchange(*r_args)

    def own_backward(n, carry):
        backward(n, (0,), [eown[n, 0:1, :]], False)
        return carry

    lax.fori_loop(0, NETS, own_backward, 0)
    hear(2, (0,))
    ar_start(1, ar_finish(0))

    arrive(*r_args)
    for n in range(NETS):
        b, c = n // 2, n % 2
        first = choose(
            [
                rin[0, n : n + 1, :],
                rin[1, n : n + 1, :],
                rbuf[0, n + 2 : n + 3, :] if b == 0 else rin[2, n - 2 : n - 1, :],
                rbuf[0, n - 2 : n - 1, :] if b == 1 else rin[3, n + 2 : n + 3, :],
            ]
        )
        second = choose(
            [
                rbuf[1, n + 1 : n + 2, :] if c == 0 else rin[4, n - 1 : n, :],
                rbuf[1, n - 1 : n, :] if c == 1 else rin[5, n + 1 : n + 2, :],
                jnp.zeros((1, PTS), F32),
            ]
        )
        cols[n, 0] = jnp.broadcast_to(first, (8, PTS))
        cols[n, 1] = jnp.broadcast_to(second, (8, PTS))

    def face_backward(n, carry):
        backward(n, (1, 2), [cols[n, 0, 0:1, :], cols[n, 1, 0:1, :]], True)
        joined = []
        for ref in (acc2, acc3):
            low_rows = ref[n, 0:64, :]
            high_rows = ref[n, 64:128, :]
            joined.append(low_rows[:, 0:64] + high_rows[:, 0:64] + high_rows[:, 64:128])
        work[...] = jnp.concatenate(joined, axis=1)
        even = work[pl.ds(0, 32, stride=2), :]
        odd = work[pl.ds(1, 32, stride=2), :]
        bias2 = acc2[n, 128:129, :]
        bias3 = acc3[n, 128:129, :]
        bias2 = bias2[:, 0:64] + bias2[:, 64:128]
        bias3 = bias3[:, 0:64] + bias3[:, 64:128]
        first = acc1[n, 0:8, :] + acc1[n, 8:16, :]
        first = first[:, 0:64] + first[:, 64:128]
        last = acco[n, 0:1, :] + acco[n, 1:2, :] + acco[n, 2:3, :]
        last = last[:, 0:64] + last[:, 64:128]
        flat_out[n, 0:1, 0:64] = first[0:1]
        flat_out[n, 0:1, 64:128] = first[1:2]
        flat_out[n, 1:2, 0:64] = first[2:3]
        flat_out[n, 1:2, 64:128] = first[3:4]
        flat_out[n, 2:3, 0:64] = first[4:5]
        flat_out[n, 2:34, 64:128] = even[:, 0:64]
        flat_out[n, 3:35, 0:64] = odd[:, 0:64]
        flat_out[n, 34:35, 64:128] = bias2
        flat_out[n, 35:67, 0:64] = even[:, 64:128]
        flat_out[n, 35:67, 64:128] = odd[:, 64:128]
        flat_out[n, 67:68, 0:64] = bias3
        flat_out[n, 67:68, 64:128] = last
        return carry

    lax.fori_loop(0, NETS, face_backward, 0)
    count = NETS * sizes[0] * sizes[1] * sizes[2]
    for n in range(NETS):
        grad_out[n // 2, :, n % 2, :] = flat_out[n]
    stores = [
        pltpu.make_async_copy(near, away, out_sem.at[k])
        for k, (near, away) in enumerate(
            (
                (res_out, res_far),
                (grad_out, grad_far),
                (inner_out, inner_far),
                (outer_out, outer_far),
            )
        )
    ]
    stores[0].start()
    stores[1].start()
    for args in (g_args, e_args, r_args):
        sent(*args)
    total = ar_finish(1) * (count ** (-0.5))
    for k in range(4):
        inner_out[:, k * PTS : (k + 1) * PTS] = total[6 * k : 6 * k + 5]
        outer_out[:, k * PTS : (k + 1) * PTS] = total[6 * k + 5 : 6 * k + 6]
    stores[2].start()
    stores[3].start()
    for store in stores:
        store.wait()
    for stage in range(2):
        for out in ar_copies(stage, False):
            out.wait_send()


def writer(*refs):
    for k in range(4):
        refs[k + 4][...] = refs[k][...]


def on_device(fine_params, coarse_inner, coarse_outer, points, source, conductivity, face_points):
    sizes = tuple(lax.axis_size(axis) for axis in AXES)
    far = pl.BlockSpec(memory_space=pltpu.HBM)
    results = pl.pallas_call(
        partial(kernel, sizes),
        out_shape=(
            jax.ShapeDtypeStruct((NETS, PTS), F32),
            jax.ShapeDtypeStruct((2, ROWS, 2, PTS), F32),
            jax.ShapeDtypeStruct((5, COARSE), F32),
            jax.ShapeDtypeStruct((1, COARSE), F32),
        ),
        in_specs=[far] * 7,
        out_specs=(far,) * 4,
        scratch_shapes=[
            pltpu.VMEM((NETS, PTS), F32),
            pltpu.VMEM((2, ROWS, 2, PTS), F32),
            pltpu.VMEM((5, COARSE), F32),
            pltpu.VMEM((1, COARSE), F32),
            pltpu.SemaphoreType.DMA((4,)),
            pltpu.VMEM((2, ROWS, 2, PTS), F32),
            pltpu.VMEM((5, COARSE), F32),
            pltpu.VMEM((1, COARSE), F32),
            pltpu.VMEM((NETS, 4, PTS), F32),
            pltpu.VMEM((NETS, PTS), F32),
            pltpu.VMEM((2, 2), F32),
            pltpu.VMEM((2, 6, 2, FACE), jnp.int32),
            pltpu.SemaphoreType.DMA((7,)),
            pltpu.VMEM((NETS, PTS, 2 * PTS), BF),
            pltpu.VMEM((2, NETS, 8, PTS), F32),
            pltpu.VMEM((6, NETS, 8, PTS), F32),
            pltpu.VMEM((2, 8, PTS), F32),
            pltpu.VMEM((6, 8, PTS), F32),
            pltpu.VMEM((2, 8, PTS), F32),
            pltpu.VMEM((6, 8, PTS), F32),
            pltpu.VMEM((NETS, 3, 8, PTS), F32),
            pltpu.VMEM((NETS, 2, 8, PTS), F32),
            pltpu.VMEM((NETS, 8, HID, PTS), F32),
            pltpu.VMEM((NETS, HID, PTS), F32),
            pltpu.VMEM((NETS, 2, HID, 3 * HID), BF),
            pltpu.VMEM((NETS, 2, HID, 3 * HID), BF),
            pltpu.VMEM((NETS, 208, 3 * WIDTH), BF),
            pltpu.VMEM((NETS, 208, 3 * WIDTH), BF),
            pltpu.VMEM((NETS, HID, 3 * PTS), F32),
            pltpu.VMEM((NETS, HID, 3 * WIDTH), F32),
            pltpu.VMEM((NETS, HID, 3 * WIDTH), F32),
            pltpu.VMEM((NETS, PTS, 3 * PTS), BF),
            pltpu.VMEM((3, 192, 3 * WIDTH), BF),
            pltpu.VMEM((NETS, 144, PTS), F32),
            pltpu.VMEM((NETS, 144, PTS), F32),
            pltpu.VMEM((NETS, 16, PTS), F32),
            pltpu.VMEM((NETS, 16, PTS), F32),
            pltpu.VMEM((HID, PTS), F32),
            pltpu.VMEM((NETS, 8, PTS), F32),
            pltpu.VMEM((2, COARSE, PTS), F32),
            pltpu.VMEM((4, COARSE, 10 * PTS), BF),
            pltpu.VMEM((COARSE, 10 * PTS), F32),
            pltpu.VMEM((3, 16, COARSE), F32),
            pltpu.VMEM((2, 16, 24, PTS), F32),
            pltpu.SemaphoreType.DMA((6,)),
            pltpu.SemaphoreType.DMA((6,)),
            pltpu.SemaphoreType.DMA((6,)),
            pltpu.SemaphoreType.DMA((6,)),
            pltpu.SemaphoreType.DMA((6,)),
            pltpu.SemaphoreType.DMA((6,)),
            pltpu.SemaphoreType.DMA((2, 16)),
            pltpu.SemaphoreType.DMA((2, 16)),
            pltpu.SemaphoreType.REGULAR((3, 6)),
            pltpu.VMEM((NETS, ROWS, PTS), F32),
        ],
        compiler_params=pltpu.CompilerParams(
            collective_id=0, has_side_effects=True, vmem_limit_bytes=63 * 1024 * 1024
        ),
    )(
        fine_params.reshape(2, 2, ROWS, PTS).transpose(0, 2, 1, 3),
        coarse_inner,
        coarse_outer.reshape(1, COARSE),
        points.reshape(NETS, 4, PTS),
        source.reshape(NETS, PTS),
        conductivity.reshape(2, 2),
        face_points.transpose(0, 1, 3, 2, 4).reshape(2, 6, 2, FACE),
    )
    residual, grads, inner_grads, outer_grads = pl.pallas_call(
        writer,
        out_shape=tuple(jax.ShapeDtypeStruct(value.shape, F32) for value in results),
        in_specs=[pl.BlockSpec(memory_space=pltpu.VMEM)] * 4,
        out_specs=(pl.BlockSpec(memory_space=pltpu.VMEM),) * 4,
        compiler_params=pltpu.CompilerParams(vmem_limit_bytes=63 * 1024 * 1024),
    )(*results)
    return (
        residual.reshape(source.shape),
        grads.transpose(0, 2, 1, 3).reshape(fine_params.shape),
        inner_grads,
        outer_grads.reshape(COARSE),
    )


def solution(mesh):
    return jax.shard_map(
        on_device,
        mesh=mesh,
        in_specs=(
            P("gx", "gy", "gz", None),
            P(),
            P(),
            P("gx", "gy", "gz", None, None),
            P("gx", "gy", "gz", None),
            P("gx", "gy", "gz"),
            P("gx", "gy", "gz", None, None),
        ),
        out_specs=(P("gx", "gy", "gz", None), P("gx", "gy", "gz", None), P(), P()),
        check_vma=False,
    )
```

```python
from functools import partial

import jax
import jax.numpy as jnp
from jax import lax
from jax.experimental import pallas as pl
from jax.experimental.pallas import tpu as pltpu
from jax.sharding import PartitionSpec as P

PTS = 128
FACE = 32
HID = 64
COARSE = 512
ROWS = 68
NETS = 4
CH = 6
WIDTH = CH * PTS
AXES = ("gx", "gy", "gz")
MESH = pl.DeviceIdType.MESH
BF = jnp.bfloat16
F32 = jnp.float32


def split2(x):
    hi = x.astype(BF)
    return hi, (x - hi.astype(F32)).astype(BF)


def split3(x):
    hi = x.astype(BF)
    rest = x - hi.astype(F32)
    mid = rest.astype(BF)
    return hi, mid, (rest - mid.astype(F32)).astype(BF)


def dot(a, b):
    return lax.dot_general(a, b, (((1,), (0,)), ((), ())), preferred_element_type=F32)


def dot_nt(a, b):
    return lax.dot_general(a, b, (((1,), (1,)), ((), ())), preferred_element_type=F32)


def iota(shape, dim):
    return lax.broadcasted_iota(jnp.int32, shape, dim)


def stacked3(row):
    which = iota((16, row.shape[1]), 0)
    hi = row.astype(BF).astype(F32)
    rest = row - hi
    mid = rest.astype(BF).astype(F32)
    low = rest - mid
    rows = jnp.where(which == 0, hi, jnp.where(which == 1, mid, jnp.where(which == 2, low, 0.0)))
    return rows.astype(BF)


def coefficients(x):
    sx, sy, sz, kappa = x[0:1], x[1:2], x[2:3], x[4:5]
    square = sx * sx + sy * sy + sz * sz
    window = jnp.exp(-square)
    scaled = kappa * window
    return (
        scaled * (6.0 - 4.0 * square),
        4.0 * scaled * sx,
        4.0 * scaled * sy,
        4.0 * scaled * sz,
        2.0 * window,
        -scaled,
    )


def kernel(
    sizes,
    params_hbm,
    inner_hbm,
    outer_hbm,
    points_hbm,
    source_hbm,
    kappa_hbm,
    faces_hbm,
    res_far,
    grad_far,
    inner_far,
    outer_far,
    res_out,
    grad_out,
    inner_out,
    outer_out,
    out_sem,
    params,
    inner,
    outer,
    points,
    source,
    kappa,
    faces,
    in_sem,
    hot,
    gbuf,
    gin,
    ebuf,
    ein,
    rbuf,
    rin,
    xs,
    cols,
    wide,
    wsq,
    lf,
    lb,
    act1,
    act2,
    hid1,
    state2,
    state3,
    qs,
    dz,
    acc3,
    acc2,
    acc1,
    acco,
    work,
    eown,
    ccols,
    cact,
    cone,
    ccurve,
    csums,
    ar,
    g_send,
    g_recv,
    e_send,
    e_recv,
    r_send,
    r_recv,
    ar_send,
    ar_recv,
    tokens,
    flat_out,
):
    place = [lax.axis_index(axis) for axis in AXES]
    def target(slot, flip):
        axis = slot // 2
        sign = (2 * (slot % 2) - 1) * (-1 if flip else 1)
        return AXES[axis], place[axis] + sign, sizes[axis]

    groups = [
        (
            place[1] * sizes[2] + place[2],
            sizes[1] * sizes[2],
            lambda p: {"gy": p // sizes[2], "gz": lax.rem(p, sizes[2])},
        ),
        (place[0], sizes[0], lambda p: {"gx": p}),
    ]

    def ring(axis, step):
        return {AXES[axis]: lax.rem(place[axis] + step + sizes[axis], sizes[axis])}

    def pass_on(level, axes):
        for axis in axes:
            reach = (1 << level) if axis == 0 else 1
            for side in range(2):
                pl.semaphore_signal(
                    tokens.at[level, 2 * axis + side],
                    inc=1,
                    device_id=ring(axis, reach if side else -reach),
                    device_id_type=MESH,
                )

    def hear(level, axes):
        for axis in axes:
            for side in range(2):
                pl.semaphore_wait(tokens.at[level, 2 * axis + side], 1)

    def exchange(source_of, landing, send_sem, recv_sem, flip):
        for slot in range(6):
            axis, where, size = target(slot, flip)

            @pl.when(jnp.logical_and(where >= 0, where < size))
            def _(slot=slot, axis=axis, where=where):
                pltpu.make_async_remote_copy(
                    source_of(slot), landing.at[slot], send_sem.at[slot], recv_sem.at[slot],
                    device_id={axis: where}, device_id_type=MESH,
                ).start()

    def arrive(source_of, landing, send_sem, recv_sem, flip):
        for slot in range(6):
            axis, where, size = target(slot, not flip)

            @pl.when(jnp.logical_and(where >= 0, where < size))
            def _(slot=slot, axis=axis, where=where):
                pltpu.make_async_remote_copy(
                    source_of(slot), landing.at[slot], send_sem.at[slot], recv_sem.at[slot],
                    device_id={axis: where}, device_id_type=MESH,
                ).wait_recv()

    def sent(source_of, landing, send_sem, recv_sem, flip):
        for slot in range(6):
            axis, where, size = target(slot, flip)

            @pl.when(jnp.logical_and(where >= 0, where < size))
            def _(slot=slot, axis=axis, where=where):
                pltpu.make_async_remote_copy(
                    source_of(slot), landing.at[slot], send_sem.at[slot], recv_sem.at[slot],
                    device_id={axis: where}, device_id_type=MESH,
                ).wait_send()

    def ar_copies(stage, arriving):
        pos, size, member = groups[stage]
        for k in range(1, size):
            partner = lax.rem(pos + k, size)
            slot = partner if arriving else pos
            yield pltpu.make_async_remote_copy(
                ar.at[stage, pos], ar.at[stage, slot],
                ar_send.at[stage, partner], ar_recv.at[stage, slot],
                device_id=member(partner), device_id_type=MESH,
            )

    def ar_start(stage, value):
        ar[stage, groups[stage][0]] = value
        for out in ar_copies(stage, False):
            out.start()

    def ar_finish(stage):
        for back in ar_copies(stage, True):
            back.wait_recv()
        total = ar[stage, 0]
        for p in range(1, groups[stage][1]):
            total = total + ar[stage, p]
        return total

    gin[...] = jnp.zeros_like(gin)
    ein[...] = jnp.zeros_like(ein)
    rin[...] = jnp.zeros_like(rin)

    barrier = pltpu.get_barrier_semaphore()
    for axis in range(3):
        for step in (-1, 1):
            pl.semaphore_signal(barrier, inc=1, device_id=ring(axis, step), device_id_type=MESH)

    fetches = [
        pltpu.make_async_copy(far, near, in_sem.at[k])
        for k, (far, near) in enumerate(
            (
                (points_hbm, points),
                (faces_hbm, faces),
                (kappa_hbm, kappa),
                (params_hbm, params),
                (inner_hbm, inner),
                (outer_hbm, outer),
                (source_hbm, source),
            )
        )
    ]
    for fetch in fetches:
        fetch.start()

    lane = iota((1, PTS), 1)
    row8 = iota((8, PTS), 0)
    group = lane // FACE
    for fetch in fetches[0:3]:
        fetch.wait()
    for j in range(NETS):
        b, c = j // 2, j % 2
        index = [faces[b, k, c : c + 1, :] for k in range(6)]
        first = jnp.concatenate(index[0:4], axis=1)
        second = jnp.concatenate(index[4:6] + [jnp.full((1, 2 * FACE), -1, jnp.int32)], axis=1)
        point = iota((PTS, PTS), 0)
        hot[j, :, 0:PTS] = jnp.where(point == first, 1.0, 0.0).astype(BF)
        hot[j, :, PTS : 2 * PTS] = jnp.where(point == second, 1.0, 0.0).astype(BF)
        own = jnp.concatenate([points[j], jnp.zeros((4, PTS), F32)], axis=0)
        own = jnp.where(row8 == 4, kappa[b : b + 1, c : c + 1], own)
        own = jnp.where(row8 == 5, 1.0, own)
        xs[j, 0] = own
        hi, mid, low_part = split3(own)
        pieces = jnp.concatenate([hi, mid, low_part, jnp.zeros_like(hi)], axis=0)
        moved = dot(pieces, hot[j])
        moved = moved[0:8] + moved[8:16] + moved[16:24]
        shift_a = jnp.where(row8 == group // 2, (2 * (group % 2) - 1).astype(F32), 0.0)
        shift_b = jnp.where(row8 == 2, jnp.where(group < 2, (2 * (group % 2) - 1).astype(F32), 0.0), 0.0)
        gbuf[0, j] = moved[:, 0:PTS] - shift_a
        gbuf[1, j] = moved[:, PTS : 2 * PTS] - shift_b

    pl.semaphore_wait(barrier, 6)
    g_args = (lambda slot: gbuf.at[slot // 4], gin, g_send, g_recv, False)
    exchange(*g_args)
    pass_on(0, (0, 1, 2))

    for fetch in fetches[3:]:
        fetch.wait()
    half = iota((32, PTS), 1) < HID
    for n in range(NETS):
        flat = params[n // 2, :, n % 2, :]
        even = pltpu.roll(jnp.where(half, flat[35:67], flat[2:34]), HID, 1)
        odd = jnp.where(half, flat[3:35], flat[35:67])
        work[pl.ds(0, 32, stride=2), :] = even
        work[pl.ds(1, 32, stride=2), :] = odd
        both = work[...]
        hi, lo = split2(both)
        lb[n, 0, :, 0:64] = hi[:, 0:64]
        lb[n, 0, :, 64:128] = hi[:, 0:64]
        lb[n, 0, :, 128:192] = lo[:, 0:64]
        lb[n, 1, :, 0:64] = hi[:, 64:128]
        lb[n, 1, :, 64:128] = hi[:, 64:128]
        lb[n, 1, :, 128:192] = lo[:, 64:128]
        hi, lo = split2(both.T)
        for layer in range(2):
            lf[n, layer, :, 0:64] = hi[64 * layer : 64 * layer + 64]
            lf[n, layer, :, 64:128] = hi[64 * layer : 64 * layer + 64]
            lf[n, layer, :, 128:192] = lo[64 * layer : 64 * layer + 64]
        vectors = jnp.concatenate(
            [
                flat[0:1],
                pltpu.roll(flat[0:1], HID, 1),
                flat[1:2],
                pltpu.roll(flat[1:2], HID, 1),
                flat[2:3],
                pltpu.roll(flat[34:35], HID, 1),
                flat[67:68],
                pltpu.roll(flat[67:68], HID, 1),
            ],
            axis=0,
        )
        columns = vectors.T
        for k in range(8):
            wide[n, k] = jnp.broadcast_to(columns[0:64, k : k + 1], (64, PTS))
        wsq[n] = wide[n, 0] * wide[n, 0] + wide[n, 1] * wide[n, 1] + wide[n, 2] * wide[n, 2]
        first_channel = jnp.where(
            jnp.logical_and(iota((16, PTS), 0) == 0, iota((16, PTS), 1) >= 0), 1.0, 0.0
        ).astype(BF)
        for tile in range(3):
            for k in range(CH):
                at = (tile * CH + k) * PTS
                value = first_channel if k == 0 else jnp.zeros_like(first_channel)
                act1[n, 192:208, at : at + PTS] = value
                act2[n, 192:208, at : at + PTS] = value

    def put(ref, n, at, value):
        hi, lo = split2(value)
        ref[n, 0:64, at : at + PTS] = hi
        ref[n, 64:128, at : at + PTS] = lo
        ref[n, 128:192, at : at + PTS] = hi

    def forward(n, tiles):
        begin, end = tiles[0] * WIDTH, (tiles[-1] + 1) * WIDTH
        for tile in tiles:
            x = xs[n, tile]
            pre = (
                wide[n, 4]
                + wide[n, 0] * x[0:1]
                + wide[n, 1] * x[1:2]
                + wide[n, 2] * x[2:3]
                + wide[n, 3] * x[3:4]
            )
            hidden = jnp.tanh(pre)
            one = 1.0 - hidden * hidden
            two = -2.0 * hidden * one
            hid1[n, :, tile * PTS : (tile + 1) * PTS] = hidden
            at = tile * WIDTH
            put(act1, n, at, hidden)
            for k in range(4):
                put(act1, n, at + (k + 1) * PTS, one * wide[n, k])
            put(act1, n, at + 5 * PTS, two * wsq[n])
        product = dot(lf[n, 0], act1[n, 0:192, begin:end])
        for tile in tiles:
            at = tile * WIDTH
            z = [product[:, at - begin + k * PTS : at - begin + (k + 1) * PTS] for k in range(CH)]
            hidden = jnp.tanh(z[0] + wide[n, 5])
            one = 1.0 - hidden * hidden
            two = -2.0 * hidden * one
            state2[n, :, at : at + PTS] = hidden
            for k in range(1, CH):
                state2[n, :, at + k * PTS : at + (k + 1) * PTS] = z[k]
            put(act2, n, at, hidden)
            for k in range(1, 5):
                put(act2, n, at + k * PTS, one * z[k])
            put(act2, n, at + 5 * PTS, two * (z[1] * z[1] + z[2] * z[2] + z[3] * z[3]) + one * z[5])
        product = dot(lf[n, 1], act2[n, 0:192, begin:end])
        results = []
        for tile in tiles:
            at = tile * WIDTH
            z = [product[:, at - begin + k * PTS : at - begin + (k + 1) * PTS] for k in range(CH)]
            coef = coefficients(xs[n, tile])
            hidden = jnp.tanh(z[0] + wide[n, 6])
            one = 1.0 - hidden * hidden
            two = -2.0 * hidden * one
            mixed = coef[5] * z[5]
            for k in range(1, 5):
                mixed = mixed + coef[k] * z[k]
            curved = coef[5] * (z[1] * z[1] + z[2] * z[2] + z[3] * z[3])
            q = coef[0] * hidden + one * mixed + two * curved
            state3[n, :, at : at + PTS] = hidden
            for k in range(1, 4):
                state3[n, :, at + k * PTS : at + (k + 1) * PTS] = z[k]
            state3[n, :, at + 4 * PTS : at + 5 * PTS] = mixed
            state3[n, :, at + 5 * PTS : at + 6 * PTS] = q
            results.append(jnp.sum(wide[n, 7] * q, axis=0, keepdims=True))
        return results

    def backward(n, tiles, rows, add):
        begin, end = tiles[0] * WIDTH, (tiles[-1] + 1) * WIDTH

        def collect(ref, value):
            ref[n] = ref[n] + value if add else value

        for tile, row in zip(tiles, rows):
            at = tile * WIDTH
            coef = [value * row for value in coefficients(xs[n, tile])]
            hidden, z1, z2, z3, mixed, q = (
                state3[n, :, at + k * PTS : at + (k + 1) * PTS] for k in range(CH)
            )
            hi, lo = split2(q)
            qs[n, 0:64, tile * PTS : (tile + 1) * PTS] = hi
            qs[n, 64:128, tile * PTS : (tile + 1) * PTS] = lo
            squared = hidden * hidden
            one = 1.0 - squared
            three = -2.0 * one * (1.0 - 3.0 * squared)
            out = wide[n, 7]
            one = out * one
            two = -2.0 * hidden * one
            curved = coef[5] * (z1 * z1 + z2 * z2 + z3 * z3)
            put(dz, 0, at, coef[0] * one + two * (mixed * row) + (out * three) * curved)
            twice = 2.0 * coef[5] * two
            for k, z in ((1, z1), (2, z2), (3, z3)):
                put(dz, 0, at + k * PTS, coef[k] * one + twice * z)
            put(dz, 0, at + 4 * PTS, coef[4] * one)
            put(dz, 0, at + 5 * PTS, coef[5] * one)
        product = dot(lb[n, 1], dz[0, 0:192, begin:end])
        collect(acc3, dot_nt(act2[n, 64:208, begin:end], dz[0, 0:128, begin:end]))
        row = jnp.concatenate(rows, axis=1)
        span = slice(tiles[0] * PTS, (tiles[-1] + 1) * PTS)
        collect(acco, dot_nt(stacked3(row), qs[n, :, span]))
        for tile in tiles:
            at = tile * WIDTH
            a = [product[:, at - begin + k * PTS : at - begin + (k + 1) * PTS] for k in range(CH)]
            z = [state2[n, :, at + k * PTS : at + (k + 1) * PTS] for k in range(CH)]
            squared = z[0] * z[0]
            one = 1.0 - squared
            two = -2.0 * z[0] * one
            three = -2.0 * one * (1.0 - 3.0 * squared)
            mixed = z[5] * a[5]
            for k in range(1, 5):
                mixed = mixed + z[k] * a[k]
            curved = (z[1] * z[1] + z[2] * z[2] + z[3] * z[3]) * a[5]
            put(dz, 1, at, one * a[0] + two * mixed + three * curved)
            twice = 2.0 * two * a[5]
            for k in range(1, 4):
                put(dz, 1, at + k * PTS, one * a[k] + twice * z[k])
            put(dz, 1, at + 4 * PTS, one * a[4])
            put(dz, 1, at + 5 * PTS, one * a[5])
        product = dot(lb[n, 0], dz[1, 0:192, begin:end])
        collect(acc2, dot_nt(act1[n, 64:208, begin:end], dz[1, 0:128, begin:end]))
        total = None
        for tile in tiles:
            at = tile * WIDTH
            a = [product[:, at - begin + k * PTS : at - begin + (k + 1) * PTS] for k in range(CH)]
            hidden = hid1[n, :, tile * PTS : (tile + 1) * PTS]
            squared = hidden * hidden
            one = 1.0 - squared
            two = -2.0 * hidden * one
            three = -2.0 * one * (1.0 - 3.0 * squared)
            mixed = wide[n, 0] * a[1]
            for k in range(1, 4):
                mixed = mixed + wide[n, k] * a[k + 1]
            twice = 2.0 * two * a[5]
            base = tile * WIDTH
            put(dz, 2, base, one * a[0] + two * mixed + three * (wsq[n] * a[5]))
            for k in range(3):
                put(dz, 2, base + (k + 1) * PTS, one * a[k + 1] + twice * wide[n, k])
            put(dz, 2, base + 4 * PTS, one * a[4])
            x = xs[n, tile]
            hi = x.astype(BF).astype(F32)
            top = jnp.where(row8 < 4, hi, jnp.where(row8 == 4, 1.0, 0.0))
            bottom = jnp.where(row8 < 4, x - hi, 0.0)
            pieces = [jnp.concatenate([top, bottom], axis=0)]
            for k in range(4):
                pieces.append(jnp.where(iota((16, PTS), 0) == k, 1.0, 0.0))
            left = jnp.concatenate(pieces, axis=1).astype(BF)
            part = dot_nt(left, dz[2, 0:128, base : base + 5 * PTS])
            total = part if total is None else total + part
        collect(acc1, total)

    def own_forward(n, carry):
        eown[n] = jnp.broadcast_to(forward(n, (0,))[0], (8, PTS))
        return carry

    lax.fori_loop(0, NETS, own_forward, 0, unroll=4)

    scales = (2.0 / sizes[0], 2.0 / (2 * sizes[1]), 2.0 / (2 * sizes[2]))
    ci = inner[...]
    co = outer[...]
    squares = (
        ci[0:1] * ci[0:1] * (scales[0] * scales[0])
        + ci[1:2] * ci[1:2] * (scales[1] * scales[1])
        + ci[2:3] * ci[2:3] * (scales[2] * scales[2])
    )
    pad = jnp.zeros((3, COARSE), F32)
    c8 = jnp.concatenate([ci, pad], axis=0)
    hi = c8.astype(BF).astype(F32)
    mid = (c8 - hi).astype(BF).astype(F32)
    lo = c8 - hi - mid
    fronts = jnp.concatenate([hi, hi, mid, hi, lo, mid], axis=0).T.astype(BF)
    two_rows = jnp.concatenate(
        [2.0 * co * ci[3:4], 2.0 * co * squares, jnp.zeros((6, COARSE), F32)], axis=0
    ).T
    ccols[0] = jnp.broadcast_to(two_rows[:, 0:1], (COARSE, PTS))
    ccols[1] = jnp.broadcast_to(two_rows[:, 1:2], (COARSE, PTS))
    ccols[2] = 2.0 * ccols[0]

    def coarse_inputs(n, x):
        b, c = n // 2, n % 2
        centres = (
            place[0].astype(F32) + 0.5,
            (2 * place[1] + b).astype(F32) + 0.5,
            (2 * place[2] + c).astype(F32) + 0.5,
        )
        v = jnp.where(row8 == 3, x, 0.0)
        for k in range(3):
            v = jnp.where(row8 == k, (centres[k] + x) * scales[k] - 1.0, v)
        return jnp.where(row8 == 4, 1.0, v)

    def coarse_forward(block, v, conductivity, wanted):
        hi = v.astype(BF).astype(F32)
        mid = (v - hi).astype(BF).astype(F32)
        lo = v - hi - mid
        backs = jnp.concatenate([hi, mid, hi, lo, hi, mid], axis=0).astype(BF)
        hidden = jnp.tanh(dot(fronts, backs))
        squared = hidden * hidden
        one = 1.0 - squared
        curve = one * hidden
        level = ccols[1] * conductivity
        slope = level * (one * (1.0 - 3.0 * squared)) - ccols[2] * curve
        at = slice(block * PTS, (block + 1) * PTS)
        cone[:, at] = one
        ccurve[:, at] = curve
        hi, lo = split2(slope)
        cact[0, :, at] = hi
        cact[1, :, at] = lo
        if wanted:
            return jnp.sum(ccols[0] * one + level * curve, axis=0, keepdims=True)

    def coarse_sums(blocks, first):
        lefts = []
        for weight, v, _ in blocks:
            plain = weight * v
            hi = plain.astype(BF).astype(F32)
            lefts.append(jnp.concatenate([hi, plain - hi], axis=0))
        left = jnp.concatenate(lefts, axis=1).astype(BF)
        span = slice(first * PTS, (first + len(blocks)) * PTS)
        upper = dot_nt(left, cact[0, :, span])
        lower = dot_nt(left, cact[1, :, span])
        sums = [upper[0:8] + upper[8:16] + lower[0:8]]
        ones = jnp.ones((16, PTS), BF)
        for ref, powers in ((cone, 0), (ccurve, 1)):
            weighted = None
            for k, (weight, _, conductivity) in enumerate(blocks):
                factor = weight * conductivity if powers else weight
                term = ref[:, (first + k) * PTS : (first + k + 1) * PTS] * factor
                weighted = term if weighted is None else weighted + term
            hi, lo = split2(weighted)
            sums.append((dot_nt(ones, hi) + dot_nt(ones, lo))[0:8])
        return sums

    blocks = []
    for j in range(NETS):
        x = xs[j, 0]
        v = coarse_inputs(j, x)
        base = eown[j, 0:1, :] + coarse_forward(j, v, x[4:5], True) - source[j : j + 1, :]
        eown[j, 0:1, :] = base
        blocks.append((base * (1.0 / PTS), v, x[4:5]))
    own_sums = coarse_sums(blocks, 0)
    for k in range(3):
        csums[k] = own_sums[k]

    hear(0, (0, 1, 2))
    pass_on(1, (0, 1, 2))

    arrive(*g_args)
    def choose(parts):
        picked = parts[-1]
        for k in range(len(parts) - 2, -1, -1):
            picked = jnp.where(group == k, parts[k], picked)
        return picked

    blank = jnp.zeros((8, PTS), F32)
    for n in range(NETS):
        b, c = n // 2, n % 2
        slots = [
            gin[0, n],
            gin[1, n],
            gbuf[0, n + 2] if b == 0 else gin[2, n - 2],
            gbuf[0, n - 2] if b == 1 else gin[3, n + 2],
        ]
        xs[n, 1] = choose(slots)
        slots = [
            gbuf[1, n + 1] if c == 0 else gin[4, n - 1],
            gbuf[1, n - 1] if c == 1 else gin[5, n + 1],
            blank,
        ]
        xs[n, 2] = choose(slots)

    def face_forward(n, carry):
        first, second = forward(n, (1, 2))
        ebuf[0, pl.ds(n, 1), :] = first
        ebuf[1, pl.ds(n, 1), :] = second
        return carry

    ebuf[...] = jnp.zeros_like(ebuf)
    lax.fori_loop(0, 2, face_forward, 0, unroll=2)
    hear(1, (1, 2))
    pass_on(2, (1, 2))
    lax.fori_loop(2, NETS, face_forward, 0, unroll=2)
    e_args = (lambda slot: ebuf.at[slot // 4], ein, e_send, e_recv, True)
    exchange(*e_args)

    hear(1, (0,))
    pass_on(2, (0,))
    def joined_halves(first, second):
        return jnp.where(lane < HID, first, pltpu.roll(second, HID, 1))

    weights, inputs, levels = [], [], []
    for n in range(NETS):
        for tile in range(2):
            x = xs[n, tile + 1]
            weights.append(ebuf[tile, n : n + 1, :] * x[5:6] * (1.0 / PTS))
            inputs.append(coarse_inputs(n, x))
            levels.append(x[4:5])
    blocks = [(weights[2 * n], inputs[2 * n], levels[2 * n]) for n in range(NETS)]
    for n in range(0, NETS, 2):
        blocks.append(
            tuple(
                joined_halves(values[2 * n + 1], values[2 * n + 3])
                for values in (weights, inputs, levels)
            )
        )
    for k, (_, v, level) in enumerate(blocks):
        coarse_forward(NETS + k, v, level, False)
    sums = [csums[k] + part for k, part in enumerate(coarse_sums(blocks, NETS))]
    moments, s_one, s_curve = sums[0][0:5], sums[1][0:1], sums[2][0:1]
    extra = jnp.concatenate(
        [
            (4.0 * scales[0] * scales[0]) * ci[0:1] * co * s_curve,
            (4.0 * scales[1] * scales[1]) * ci[1:2] * co * s_curve,
            (4.0 * scales[2] * scales[2]) * ci[2:3] * co * s_curve,
            2.0 * co * s_one,
            jnp.zeros((1, COARSE), F32),
        ],
        axis=0,
    )
    outer_grad = 2.0 * ci[3:4] * s_one + 2.0 * squares * s_curve
    partial_sums = jnp.concatenate([moments + extra, outer_grad], axis=0)
    hear(2, (1, 2))
    ar_start(
        0,
        jnp.concatenate([partial_sums[:, k * PTS : (k + 1) * PTS] for k in range(4)], axis=0),
    )

    arrive(*e_args)
    for j in range(NETS):
        b, c = j // 2, j % 2

        def row(ref, k):
            return ref[k : k + 1, :]

        first = choose(
            [
                row(ein.at[0], j),
                row(ein.at[1], j),
                row(ebuf.at[0], j - 2) if b == 1 else row(ein.at[2], j + 2),
                row(ebuf.at[0], j + 2) if b == 0 else row(ein.at[3], j - 2),
            ]
        )
        second = choose(
            [
                row(ebuf.at[1], j - 1) if c == 1 else row(ein.at[4], j + 1),
                row(ebuf.at[1], j + 1) if c == 0 else row(ein.at[5], j - 1),
                jnp.zeros((1, PTS), F32),
            ]
        )
        spread = dot_nt(stacked3(jnp.concatenate([first, second], axis=1)), hot[j])
        residual = eown[j, 0:1, :] + spread[0:1] + spread[1:2] + spread[2:3]
        res_out[j : j + 1, :] = residual
        scaled = residual * (1.0 / PTS)
        eown[j] = jnp.broadcast_to(scaled, (8, PTS))
        moved = dot(stacked3(scaled), hot[j])
        moved = moved[0:1] + moved[1:2] + moved[2:3]
        rbuf[0, j : j + 1, :] = moved[:, 0:PTS]
        rbuf[1, j : j + 1, :] = moved[:, PTS : 2 * PTS]
    rbuf[:, 4:8, :] = jnp.zeros((2, 4, PTS), F32)
    r_args = (lambda slot: rbuf.at[slot // 4], rin, r_send, r_recv, False)
    exchange(*r_args)

    def own_backward(n, carry):
        backward(n, (0,), [eown[n, 0:1, :]], False)
        return carry

    lax.fori_loop(0, NETS, own_backward, 0, unroll=4)
    hear(2, (0,))
    ar_start(1, ar_finish(0))

    arrive(*r_args)
    for n in range(NETS):
        b, c = n // 2, n % 2
        first = choose(
            [
                rin[0, n : n + 1, :],
                rin[1, n : n + 1, :],
                rbuf[0, n + 2 : n + 3, :] if b == 0 else rin[2, n - 2 : n - 1, :],
                rbuf[0, n - 2 : n - 1, :] if b == 1 else rin[3, n + 2 : n + 3, :],
            ]
        )
        second = choose(
            [
                rbuf[1, n + 1 : n + 2, :] if c == 0 else rin[4, n - 1 : n, :],
                rbuf[1, n - 1 : n, :] if c == 1 else rin[5, n + 1 : n + 2, :],
                jnp.zeros((1, PTS), F32),
            ]
        )
        cols[n, 0] = jnp.broadcast_to(first, (8, PTS))
        cols[n, 1] = jnp.broadcast_to(second, (8, PTS))

    def face_backward(n, carry):
        backward(n, (1, 2), [cols[n, 0, 0:1, :], cols[n, 1, 0:1, :]], True)
        joined = []
        for ref in (acc2, acc3):
            low_rows = ref[n, 0:64, :]
            high_rows = ref[n, 64:128, :]
            joined.append(low_rows[:, 0:64] + high_rows[:, 0:64] + high_rows[:, 64:128])
        work[...] = jnp.concatenate(joined, axis=1)
        even = work[pl.ds(0, 32, stride=2), :]
        odd = work[pl.ds(1, 32, stride=2), :]
        bias2 = acc2[n, 128:129, :]
        bias3 = acc3[n, 128:129, :]
        bias2 = bias2[:, 0:64] + bias2[:, 64:128]
        bias3 = bias3[:, 0:64] + bias3[:, 64:128]
        first = acc1[n, 0:8, :] + acc1[n, 8:16, :]
        first = first[:, 0:64] + first[:, 64:128]
        last = acco[n, 0:1, :] + acco[n, 1:2, :] + acco[n, 2:3, :]
        last = last[:, 0:64] + last[:, 64:128]
        flat_out[n, 0:1, 0:64] = first[0:1]
        flat_out[n, 0:1, 64:128] = first[1:2]
        flat_out[n, 1:2, 0:64] = first[2:3]
        flat_out[n, 1:2, 64:128] = first[3:4]
        flat_out[n, 2:3, 0:64] = first[4:5]
        flat_out[n, 2:34, 64:128] = even[:, 0:64]
        flat_out[n, 3:35, 0:64] = odd[:, 0:64]
        flat_out[n, 34:35, 64:128] = bias2
        flat_out[n, 35:67, 0:64] = even[:, 64:128]
        flat_out[n, 35:67, 64:128] = odd[:, 64:128]
        flat_out[n, 67:68, 0:64] = bias3
        flat_out[n, 67:68, 64:128] = last
        return carry

    lax.fori_loop(0, NETS, face_backward, 0, unroll=2)
    count = NETS * sizes[0] * sizes[1] * sizes[2]
    for n in range(NETS):
        grad_out[n // 2, :, n % 2, :] = flat_out[n]
    stores = [
        pltpu.make_async_copy(near, away, out_sem.at[k])
        for k, (near, away) in enumerate(
            (
                (res_out, res_far),
                (grad_out, grad_far),
                (inner_out, inner_far),
                (outer_out, outer_far),
            )
        )
    ]
    stores[0].start()
    stores[1].start()
    for args in (g_args, e_args, r_args):
        sent(*args)
    total = ar_finish(1) * (count ** (-0.5))
    for k in range(4):
        inner_out[:, k * PTS : (k + 1) * PTS] = total[6 * k : 6 * k + 5]
        outer_out[:, k * PTS : (k + 1) * PTS] = total[6 * k + 5 : 6 * k + 6]
    stores[2].start()
    stores[3].start()
    for store in stores:
        store.wait()
    for stage in range(2):
        for out in ar_copies(stage, False):
            out.wait_send()


def writer(*refs):
    for k in range(4):
        refs[k + 4][...] = refs[k][...]


def on_device(fine_params, coarse_inner, coarse_outer, points, source, conductivity, face_points):
    sizes = tuple(lax.axis_size(axis) for axis in AXES)
    far = pl.BlockSpec(memory_space=pltpu.HBM)
    results = pl.pallas_call(
        partial(kernel, sizes),
        out_shape=(
            jax.ShapeDtypeStruct((NETS, PTS), F32),
            jax.ShapeDtypeStruct((2, ROWS, 2, PTS), F32),
            jax.ShapeDtypeStruct((5, COARSE), F32),
            jax.ShapeDtypeStruct((1, COARSE), F32),
        ),
        in_specs=[far] * 7,
        out_specs=(far,) * 4,
        scratch_shapes=[
            pltpu.VMEM((NETS, PTS), F32),
            pltpu.VMEM((2, ROWS, 2, PTS), F32),
            pltpu.VMEM((5, COARSE), F32),
            pltpu.VMEM((1, COARSE), F32),
            pltpu.SemaphoreType.DMA((4,)),
            pltpu.VMEM((2, ROWS, 2, PTS), F32),
            pltpu.VMEM((5, COARSE), F32),
            pltpu.VMEM((1, COARSE), F32),
            pltpu.VMEM((NETS, 4, PTS), F32),
            pltpu.VMEM((NETS, PTS), F32),
            pltpu.VMEM((2, 2), F32),
            pltpu.VMEM((2, 6, 2, FACE), jnp.int32),
            pltpu.SemaphoreType.DMA((7,)),
            pltpu.VMEM((NETS, PTS, 2 * PTS), BF),
            pltpu.VMEM((2, NETS, 8, PTS), F32),
            pltpu.VMEM((6, NETS, 8, PTS), F32),
            pltpu.VMEM((2, 8, PTS), F32),
            pltpu.VMEM((6, 8, PTS), F32),
            pltpu.VMEM((2, 8, PTS), F32),
            pltpu.VMEM((6, 8, PTS), F32),
            pltpu.VMEM((NETS, 3, 8, PTS), F32),
            pltpu.VMEM((NETS, 2, 8, PTS), F32),
            pltpu.VMEM((NETS, 8, HID, PTS), F32),
            pltpu.VMEM((NETS, HID, PTS), F32),
            pltpu.VMEM((NETS, 2, HID, 3 * HID), BF),
            pltpu.VMEM((NETS, 2, HID, 3 * HID), BF),
            pltpu.VMEM((NETS, 208, 3 * WIDTH), BF),
            pltpu.VMEM((NETS, 208, 3 * WIDTH), BF),
            pltpu.VMEM((NETS, HID, 3 * PTS), F32),
            pltpu.VMEM((NETS, HID, 3 * WIDTH), F32),
            pltpu.VMEM((NETS, HID, 3 * WIDTH), F32),
            pltpu.VMEM((NETS, PTS, 3 * PTS), BF),
            pltpu.VMEM((3, 192, 3 * WIDTH), BF),
            pltpu.VMEM((NETS, 144, PTS), F32),
            pltpu.VMEM((NETS, 144, PTS), F32),
            pltpu.VMEM((NETS, 16, PTS), F32),
            pltpu.VMEM((NETS, 16, PTS), F32),
            pltpu.VMEM((HID, PTS), F32),
            pltpu.VMEM((NETS, 8, PTS), F32),
            pltpu.VMEM((3, COARSE, PTS), F32),
            pltpu.VMEM((2, COARSE, 10 * PTS), BF),
            pltpu.VMEM((COARSE, 10 * PTS), F32),
            pltpu.VMEM((COARSE, 10 * PTS), F32),
            pltpu.VMEM((3, 8, COARSE), F32),
            pltpu.VMEM((2, 16, 24, PTS), F32),
            pltpu.SemaphoreType.DMA((6,)),
            pltpu.SemaphoreType.DMA((6,)),
            pltpu.SemaphoreType.DMA((6,)),
            pltpu.SemaphoreType.DMA((6,)),
            pltpu.SemaphoreType.DMA((6,)),
            pltpu.SemaphoreType.DMA((6,)),
            pltpu.SemaphoreType.DMA((2, 16)),
            pltpu.SemaphoreType.DMA((2, 16)),
            pltpu.SemaphoreType.REGULAR((3, 6)),
            pltpu.VMEM((NETS, ROWS, PTS), F32),
        ],
        compiler_params=pltpu.CompilerParams(
            collective_id=0, has_side_effects=True, vmem_limit_bytes=63 * 1024 * 1024
        ),
    )(
        fine_params.reshape(2, 2, ROWS, PTS).transpose(0, 2, 1, 3),
        coarse_inner,
        coarse_outer.reshape(1, COARSE),
        points.reshape(NETS, 4, PTS),
        source.reshape(NETS, PTS),
        conductivity.reshape(2, 2),
        face_points.transpose(0, 1, 3, 2, 4).reshape(2, 6, 2, FACE),
    )
    residual, grads, inner_grads, outer_grads = pl.pallas_call(
        writer,
        out_shape=tuple(jax.ShapeDtypeStruct(value.shape, F32) for value in results),
        in_specs=[pl.BlockSpec(memory_space=pltpu.VMEM)] * 4,
        out_specs=(pl.BlockSpec(memory_space=pltpu.VMEM),) * 4,
        compiler_params=pltpu.CompilerParams(vmem_limit_bytes=63 * 1024 * 1024),
    )(*results)
    return (
        residual.reshape(source.shape),
        grads.transpose(0, 2, 1, 3).reshape(fine_params.shape),
        inner_grads,
        outer_grads.reshape(COARSE),
    )


def solution(mesh):
    return jax.shard_map(
        on_device,
        mesh=mesh,
        in_specs=(
            P("gx", "gy", "gz", None),
            P(),
            P(),
            P("gx", "gy", "gz", None, None),
            P("gx", "gy", "gz", None),
            P("gx", "gy", "gz"),
            P("gx", "gy", "gz", None, None),
        ),
        out_specs=(P("gx", "gy", "gz", None), P("gx", "gy", "gz", None), P(), P()),
        check_vma=False,
    )
```

```python
from functools import partial

import jax
import jax.numpy as jnp
from jax import lax
from jax.experimental import pallas as pl
from jax.experimental.pallas import tpu as pltpu
from jax.sharding import PartitionSpec as P

PTS = 128
FACE = 32
HID = 64
COARSE = 512
ROWS = 68
NETS = 4
CH = 6
WIDTH = CH * PTS
AXES = ("gx", "gy", "gz")
MESH = pl.DeviceIdType.MESH
BF = jnp.bfloat16
F32 = jnp.float32


def split2(x):
    hi = x.astype(BF)
    return hi, (x - hi.astype(F32)).astype(BF)


def split3(x):
    hi = x.astype(BF)
    rest = x - hi.astype(F32)
    mid = rest.astype(BF)
    return hi, mid, (rest - mid.astype(F32)).astype(BF)


def dot(a, b):
    return lax.dot_general(a, b, (((1,), (0,)), ((), ())), preferred_element_type=F32)


def dot_nt(a, b):
    return lax.dot_general(a, b, (((1,), (1,)), ((), ())), preferred_element_type=F32)


def iota(shape, dim):
    return lax.broadcasted_iota(jnp.int32, shape, dim)


def stacked3(row):
    which = iota((16, row.shape[1]), 0)
    hi = row.astype(BF).astype(F32)
    rest = row - hi
    mid = rest.astype(BF).astype(F32)
    low = rest - mid
    rows = jnp.where(which == 0, hi, jnp.where(which == 1, mid, jnp.where(which == 2, low, 0.0)))
    return rows.astype(BF)


def coefficients(x):
    sx, sy, sz, kappa = x[0:1], x[1:2], x[2:3], x[4:5]
    square = sx * sx + sy * sy + sz * sz
    window = jnp.exp(-square)
    scaled = kappa * window
    return (
        scaled * (6.0 - 4.0 * square),
        4.0 * scaled * sx,
        4.0 * scaled * sy,
        4.0 * scaled * sz,
        2.0 * window,
        -scaled,
    )


def kernel(
    sizes,
    params_hbm,
    inner_hbm,
    outer_hbm,
    points_hbm,
    source_hbm,
    kappa_hbm,
    faces_hbm,
    res_far,
    grad_far,
    inner_far,
    outer_far,
    res_out,
    grad_out,
    inner_out,
    outer_out,
    out_sem,
    params,
    inner,
    outer,
    points,
    source,
    kappa,
    faces,
    in_sem,
    hot,
    gbuf,
    gin,
    ebuf,
    ein,
    rbuf,
    rin,
    xs,
    cols,
    wide,
    wsq,
    lf,
    lb,
    act1,
    act2,
    hid1,
    state2,
    state3,
    qs,
    dz,
    acc3,
    acc2,
    acc1,
    acco,
    work,
    eown,
    ccols,
    cact,
    cone,
    ccurve,
    csums,
    ar,
    g_send,
    g_recv,
    e_send,
    e_recv,
    r_send,
    r_recv,
    ar_send,
    ar_recv,
    tokens,
    flat_out,
):
    place = [lax.axis_index(axis) for axis in AXES]
    def target(slot, flip):
        axis = slot // 2
        sign = (2 * (slot % 2) - 1) * (-1 if flip else 1)
        return AXES[axis], place[axis] + sign, sizes[axis]

    groups = [
        (
            place[1] * sizes[2] + place[2],
            sizes[1] * sizes[2],
            lambda p: {"gy": p // sizes[2], "gz": lax.rem(p, sizes[2])},
        ),
        (place[0], sizes[0], lambda p: {"gx": p}),
    ]

    def partners(stage):
        pos, size, _ = groups[stage]
        if sizes != (16, 4, 4):
            return [lax.rem(pos + k, size) for k in range(1, size)]
        if stage == 1:
            steps = [(2 * a + min(z, 8 - z), a, z) for a in range(2) for z in range(8)]
            return [
                lax.rem(pos // 8 + a, 2) * 8 + lax.rem(pos + z, 8)
                for hops, a, z in sorted(steps, reverse=True)
                if hops
            ]
        steps = [
            (4 * a + 4 * min(y, 4 - y) + b, a, b, y)
            for a in range(2)
            for b in range(2)
            for y in range(4)
        ]
        return [
            lax.rem(place[1] // 2 + a, 2) * 8 + lax.rem(place[1] + b, 2) * 4 + lax.rem(place[2] + y, 4)
            for hops, a, b, y in sorted(steps, reverse=True)
            if hops
        ]

    def ring(axis, step):
        return {AXES[axis]: lax.rem(place[axis] + step + sizes[axis], sizes[axis])}

    def pass_on(level):
        for side in range(2):
            pl.semaphore_signal(
                tokens.at[level, side],
                inc=1,
                device_id=ring(0, (1 << level) if side else -(1 << level)),
                device_id_type=MESH,
            )

    def hear(level):
        for side in range(2):
            pl.semaphore_wait(tokens.at[level, side], 1)

    def exchange(source_of, landing, send_sem, recv_sem, flip):
        for slot in range(6):
            axis, where, size = target(slot, flip)

            @pl.when(jnp.logical_and(where >= 0, where < size))
            def _(slot=slot, axis=axis, where=where):
                pltpu.make_async_remote_copy(
                    source_of(slot), landing.at[slot], send_sem.at[slot], recv_sem.at[slot],
                    device_id={axis: where}, device_id_type=MESH,
                ).start()

    def arrive(source_of, landing, send_sem, recv_sem, flip):
        for slot in range(6):
            axis, where, size = target(slot, not flip)

            @pl.when(jnp.logical_and(where >= 0, where < size))
            def _(slot=slot, axis=axis, where=where):
                pltpu.make_async_remote_copy(
                    source_of(slot), landing.at[slot], send_sem.at[slot], recv_sem.at[slot],
                    device_id={axis: where}, device_id_type=MESH,
                ).wait_recv()

    def sent(source_of, landing, send_sem, recv_sem, flip):
        for slot in range(6):
            axis, where, size = target(slot, flip)

            @pl.when(jnp.logical_and(where >= 0, where < size))
            def _(slot=slot, axis=axis, where=where):
                pltpu.make_async_remote_copy(
                    source_of(slot), landing.at[slot], send_sem.at[slot], recv_sem.at[slot],
                    device_id={axis: where}, device_id_type=MESH,
                ).wait_send()

    def ar_copies(stage, arriving):
        pos, _, member = groups[stage]
        for partner in partners(stage):
            slot = partner if arriving else pos
            yield pltpu.make_async_remote_copy(
                ar.at[stage, pos], ar.at[stage, slot],
                ar_send.at[stage, partner], ar_recv.at[stage, slot],
                device_id=member(partner), device_id_type=MESH,
            )

    def ar_start(stage, value):
        ar[stage, groups[stage][0]] = value
        for out in ar_copies(stage, False):
            out.start()

    def ar_finish(stage):
        for back in ar_copies(stage, True):
            back.wait_recv()
        total = ar[stage, 0]
        for p in range(1, groups[stage][1]):
            total = total + ar[stage, p]
        return total

    gin[...] = jnp.zeros_like(gin)
    ein[...] = jnp.zeros_like(ein)
    rin[...] = jnp.zeros_like(rin)

    barrier = pltpu.get_barrier_semaphore()
    for step in (-1, 1):
        pl.semaphore_signal(barrier, inc=1, device_id=ring(0, step), device_id_type=MESH)
    pos, size, member = groups[0]
    for k in range(1, size):
        pl.semaphore_signal(
            barrier, inc=1, device_id=member(lax.rem(pos + k, size)), device_id_type=MESH
        )

    fetches = [
        pltpu.make_async_copy(far, near, in_sem.at[k])
        for k, (far, near) in enumerate(
            (
                (points_hbm, points),
                (faces_hbm, faces),
                (kappa_hbm, kappa),
                (params_hbm, params),
                (inner_hbm, inner),
                (outer_hbm, outer),
                (source_hbm, source),
            )
        )
    ]
    for fetch in fetches:
        fetch.start()

    lane = iota((1, PTS), 1)
    row8 = iota((8, PTS), 0)
    group = lane // FACE
    for fetch in fetches[0:3]:
        fetch.wait()
    for j in range(NETS):
        b, c = j // 2, j % 2
        index = [faces[b, k, c : c + 1, :] for k in range(6)]
        first = jnp.concatenate(index[0:4], axis=1)
        second = jnp.concatenate(index[4:6] + [jnp.full((1, 2 * FACE), -1, jnp.int32)], axis=1)
        point = iota((PTS, PTS), 0)
        hot[j, :, 0:PTS] = jnp.where(point == first, 1.0, 0.0).astype(BF)
        hot[j, :, PTS : 2 * PTS] = jnp.where(point == second, 1.0, 0.0).astype(BF)
        own = jnp.concatenate([points[j], jnp.zeros((4, PTS), F32)], axis=0)
        own = jnp.where(row8 == 4, kappa[b : b + 1, c : c + 1], own)
        own = jnp.where(row8 == 5, 1.0, own)
        xs[j, 0] = own
        hi, mid, low_part = split3(own)
        pieces = jnp.concatenate([hi, mid, low_part, jnp.zeros_like(hi)], axis=0)
        moved = dot(pieces, hot[j])
        moved = moved[0:8] + moved[8:16] + moved[16:24]
        shift_a = jnp.where(row8 == group // 2, (2 * (group % 2) - 1).astype(F32), 0.0)
        shift_b = jnp.where(row8 == 2, jnp.where(group < 2, (2 * (group % 2) - 1).astype(F32), 0.0), 0.0)
        gbuf[0, j] = moved[:, 0:PTS] - shift_a
        gbuf[1, j] = moved[:, PTS : 2 * PTS] - shift_b

    pl.semaphore_wait(barrier, 2 + groups[0][1] - 1)
    g_args = (lambda slot: gbuf.at[slot // 4], gin, g_send, g_recv, False)
    exchange(*g_args)
    pass_on(0)

    for fetch in fetches[3:]:
        fetch.wait()
    half = iota((32, PTS), 1) < HID
    for n in range(NETS):
        flat = params[n // 2, :, n % 2, :]
        even = pltpu.roll(jnp.where(half, flat[35:67], flat[2:34]), HID, 1)
        odd = jnp.where(half, flat[3:35], flat[35:67])
        work[n, pl.ds(0, 32, stride=2), :] = even
        work[n, pl.ds(1, 32, stride=2), :] = odd
        both = work[n]
        hi, lo = split2(both)
        lb[n, 0, :, 0:64] = hi[:, 0:64]
        lb[n, 0, :, 64:128] = hi[:, 0:64]
        lb[n, 0, :, 128:192] = lo[:, 0:64]
        lb[n, 1, :, 0:64] = hi[:, 64:128]
        lb[n, 1, :, 64:128] = hi[:, 64:128]
        lb[n, 1, :, 128:192] = lo[:, 64:128]
        hi, lo = split2(both.T)
        for layer in range(2):
            lf[n, layer, :, 0:64] = hi[64 * layer : 64 * layer + 64]
            lf[n, layer, :, 64:128] = hi[64 * layer : 64 * layer + 64]
            lf[n, layer, :, 128:192] = lo[64 * layer : 64 * layer + 64]
        vectors = jnp.concatenate(
            [
                flat[0:1],
                pltpu.roll(flat[0:1], HID, 1),
                flat[1:2],
                pltpu.roll(flat[1:2], HID, 1),
                flat[2:3],
                pltpu.roll(flat[34:35], HID, 1),
                flat[67:68],
                pltpu.roll(flat[67:68], HID, 1),
            ],
            axis=0,
        )
        columns = vectors.T
        for k in range(8):
            wide[n, k] = jnp.broadcast_to(columns[0:64, k : k + 1], (64, PTS))
        wsq[n] = wide[n, 0] * wide[n, 0] + wide[n, 1] * wide[n, 1] + wide[n, 2] * wide[n, 2]
        first_channel = jnp.where(
            jnp.logical_and(iota((16, PTS), 0) == 0, iota((16, PTS), 1) >= 0), 1.0, 0.0
        ).astype(BF)
        for tile in range(3):
            for k in range(CH):
                at = (tile * CH + k) * PTS
                value = first_channel if k == 0 else jnp.zeros_like(first_channel)
                act1[n, 192:208, at : at + PTS] = value
                act2[n, 192:208, at : at + PTS] = value

    def put(ref, n, at, value):
        hi, lo = split2(value)
        ref[n, 0:64, at : at + PTS] = hi
        ref[n, 64:128, at : at + PTS] = lo
        ref[n, 128:192, at : at + PTS] = hi

    def forward(n, tiles):
        begin, end = tiles[0] * WIDTH, (tiles[-1] + 1) * WIDTH
        for tile in tiles:
            x = xs[n, tile]
            pre = (
                wide[n, 4]
                + wide[n, 0] * x[0:1]
                + wide[n, 1] * x[1:2]
                + wide[n, 2] * x[2:3]
                + wide[n, 3] * x[3:4]
            )
            hidden = jnp.tanh(pre)
            one = 1.0 - hidden * hidden
            two = -2.0 * hidden * one
            hid1[n, :, tile * PTS : (tile + 1) * PTS] = hidden
            at = tile * WIDTH
            put(act1, n, at, hidden)
            for k in range(4):
                put(act1, n, at + (k + 1) * PTS, one * wide[n, k])
            put(act1, n, at + 5 * PTS, two * wsq[n])
        product = dot(lf[n, 0], act1[n, 0:192, begin:end])
        for tile in tiles:
            at = tile * WIDTH
            z = [product[:, at - begin + k * PTS : at - begin + (k + 1) * PTS] for k in range(CH)]
            hidden = jnp.tanh(z[0] + wide[n, 5])
            one = 1.0 - hidden * hidden
            two = -2.0 * hidden * one
            state2[n, :, at : at + PTS] = hidden
            for k in range(1, CH):
                state2[n, :, at + k * PTS : at + (k + 1) * PTS] = z[k]
            put(act2, n, at, hidden)
            for k in range(1, 5):
                put(act2, n, at + k * PTS, one * z[k])
            put(act2, n, at + 5 * PTS, two * (z[1] * z[1] + z[2] * z[2] + z[3] * z[3]) + one * z[5])
        product = dot(lf[n, 1], act2[n, 0:192, begin:end])
        results = []
        for tile in tiles:
            at = tile * WIDTH
            z = [product[:, at - begin + k * PTS : at - begin + (k + 1) * PTS] for k in range(CH)]
            coef = coefficients(xs[n, tile])
            hidden = jnp.tanh(z[0] + wide[n, 6])
            one = 1.0 - hidden * hidden
            two = -2.0 * hidden * one
            mixed = coef[5] * z[5]
            for k in range(1, 5):
                mixed = mixed + coef[k] * z[k]
            curved = coef[5] * (z[1] * z[1] + z[2] * z[2] + z[3] * z[3])
            q = coef[0] * hidden + one * mixed + two * curved
            state3[n, :, at : at + PTS] = hidden
            for k in range(1, 4):
                state3[n, :, at + k * PTS : at + (k + 1) * PTS] = z[k]
            state3[n, :, at + 4 * PTS : at + 5 * PTS] = mixed
            state3[n, :, at + 5 * PTS : at + 6 * PTS] = q
            results.append(jnp.sum(wide[n, 7] * q, axis=0, keepdims=True))
        return results

    def backward(n, tiles, rows, add):
        begin, end = tiles[0] * WIDTH, (tiles[-1] + 1) * WIDTH

        def collect(ref, value):
            ref[n] = ref[n] + value if add else value

        for tile, row in zip(tiles, rows):
            at = tile * WIDTH
            coef = [value * row for value in coefficients(xs[n, tile])]
            hidden, z1, z2, z3, mixed, q = (
                state3[n, :, at + k * PTS : at + (k + 1) * PTS] for k in range(CH)
            )
            hi, lo = split2(q)
            qs[n, 0:64, tile * PTS : (tile + 1) * PTS] = hi
            qs[n, 64:128, tile * PTS : (tile + 1) * PTS] = lo
            squared = hidden * hidden
            one = 1.0 - squared
            three = -2.0 * one * (1.0 - 3.0 * squared)
            out = wide[n, 7]
            one = out * one
            two = -2.0 * hidden * one
            curved = coef[5] * (z1 * z1 + z2 * z2 + z3 * z3)
            put(dz, 3 * n + 0, at, coef[0] * one + two * (mixed * row) + (out * three) * curved)
            twice = 2.0 * coef[5] * two
            for k, z in ((1, z1), (2, z2), (3, z3)):
                put(dz, 3 * n + 0, at + k * PTS, coef[k] * one + twice * z)
            put(dz, 3 * n + 0, at + 4 * PTS, coef[4] * one)
            put(dz, 3 * n + 0, at + 5 * PTS, coef[5] * one)
        product = dot(lb[n, 1], dz[3 * n + 0, 0:192, begin:end])
        collect(acc3, dot_nt(act2[n, 64:208, begin:end], dz[3 * n + 0, 0:128, begin:end]))
        row = jnp.concatenate(rows, axis=1)
        span = slice(tiles[0] * PTS, (tiles[-1] + 1) * PTS)
        collect(acco, dot_nt(stacked3(row), qs[n, :, span]))
        for tile in tiles:
            at = tile * WIDTH
            a = [product[:, at - begin + k * PTS : at - begin + (k + 1) * PTS] for k in range(CH)]
            z = [state2[n, :, at + k * PTS : at + (k + 1) * PTS] for k in range(CH)]
            squared = z[0] * z[0]
            one = 1.0 - squared
            two = -2.0 * z[0] * one
            three = -2.0 * one * (1.0 - 3.0 * squared)
            mixed = z[5] * a[5]
            for k in range(1, 5):
                mixed = mixed + z[k] * a[k]
            curved = (z[1] * z[1] + z[2] * z[2] + z[3] * z[3]) * a[5]
            put(dz, 3 * n + 1, at, one * a[0] + two * mixed + three * curved)
            twice = 2.0 * two * a[5]
            for k in range(1, 4):
                put(dz, 3 * n + 1, at + k * PTS, one * a[k] + twice * z[k])
            put(dz, 3 * n + 1, at + 4 * PTS, one * a[4])
            put(dz, 3 * n + 1, at + 5 * PTS, one * a[5])
        product = dot(lb[n, 0], dz[3 * n + 1, 0:192, begin:end])
        collect(acc2, dot_nt(act1[n, 64:208, begin:end], dz[3 * n + 1, 0:128, begin:end]))
        total = None
        for tile in tiles:
            at = tile * WIDTH
            a = [product[:, at - begin + k * PTS : at - begin + (k + 1) * PTS] for k in range(CH)]
            hidden = hid1[n, :, tile * PTS : (tile + 1) * PTS]
            squared = hidden * hidden
            one = 1.0 - squared
            two = -2.0 * hidden * one
            three = -2.0 * one * (1.0 - 3.0 * squared)
            mixed = wide[n, 0] * a[1]
            for k in range(1, 4):
                mixed = mixed + wide[n, k] * a[k + 1]
            twice = 2.0 * two * a[5]
            base = tile * WIDTH
            put(dz, 3 * n + 2, base, one * a[0] + two * mixed + three * (wsq[n] * a[5]))
            for k in range(3):
                put(dz, 3 * n + 2, base + (k + 1) * PTS, one * a[k + 1] + twice * wide[n, k])
            put(dz, 3 * n + 2, base + 4 * PTS, one * a[4])
            x = xs[n, tile]
            hi = x.astype(BF).astype(F32)
            top = jnp.where(row8 < 4, hi, jnp.where(row8 == 4, 1.0, 0.0))
            bottom = jnp.where(row8 < 4, x - hi, 0.0)
            pieces = [jnp.concatenate([top, bottom], axis=0)]
            for k in range(4):
                pieces.append(jnp.where(iota((16, PTS), 0) == k, 1.0, 0.0))
            left = jnp.concatenate(pieces, axis=1).astype(BF)
            part = dot_nt(left, dz[3 * n + 2, 0:128, base : base + 5 * PTS])
            total = part if total is None else total + part
        collect(acc1, total)

    def own_forward(n, carry):
        eown[n] = jnp.broadcast_to(forward(n, (0,))[0], (8, PTS))
        return carry

    lax.fori_loop(0, NETS, own_forward, 0, unroll=4)

    scales = (2.0 / sizes[0], 2.0 / (2 * sizes[1]), 2.0 / (2 * sizes[2]))
    ci = inner[...]
    co = outer[...]
    squares = (
        ci[0:1] * ci[0:1] * (scales[0] * scales[0])
        + ci[1:2] * ci[1:2] * (scales[1] * scales[1])
        + ci[2:3] * ci[2:3] * (scales[2] * scales[2])
    )
    pad = jnp.zeros((3, COARSE), F32)
    c8 = jnp.concatenate([ci, pad], axis=0)
    hi = c8.astype(BF).astype(F32)
    mid = (c8 - hi).astype(BF).astype(F32)
    lo = c8 - hi - mid
    fronts = jnp.concatenate([hi, hi, mid, hi, lo, mid], axis=0).T.astype(BF)
    two_rows = jnp.concatenate(
        [2.0 * co * ci[3:4], 2.0 * co * squares, jnp.zeros((6, COARSE), F32)], axis=0
    ).T
    ccols[0] = jnp.broadcast_to(two_rows[:, 0:1], (COARSE, PTS))
    ccols[1] = jnp.broadcast_to(two_rows[:, 1:2], (COARSE, PTS))
    ccols[2] = 2.0 * ccols[0]

    def coarse_inputs(n, x):
        b, c = n // 2, n % 2
        centres = (
            place[0].astype(F32) + 0.5,
            (2 * place[1] + b).astype(F32) + 0.5,
            (2 * place[2] + c).astype(F32) + 0.5,
        )
        v = jnp.where(row8 == 3, x, 0.0)
        for k in range(3):
            v = jnp.where(row8 == k, (centres[k] + x) * scales[k] - 1.0, v)
        return jnp.where(row8 == 4, 1.0, v)

    def coarse_forward(block, v, conductivity, wanted):
        hi = v.astype(BF).astype(F32)
        mid = (v - hi).astype(BF).astype(F32)
        lo = v - hi - mid
        backs = jnp.concatenate([hi, mid, hi, lo, hi, mid], axis=0).astype(BF)
        hidden = jnp.tanh(dot(fronts, backs))
        squared = hidden * hidden
        one = 1.0 - squared
        curve = one * hidden
        level = ccols[1] * conductivity
        slope = level * (one * (1.0 - 3.0 * squared)) - ccols[2] * curve
        at = slice(block * PTS, (block + 1) * PTS)
        cone[:, at] = one
        ccurve[:, at] = curve
        hi, lo = split2(slope)
        cact[0, :, at] = hi
        cact[1, :, at] = lo
        if wanted:
            return jnp.sum(ccols[0] * one + level * curve, axis=0, keepdims=True)

    def coarse_sums(blocks, first):
        lefts = []
        for weight, v, _ in blocks:
            plain = weight * v
            hi = plain.astype(BF).astype(F32)
            lefts.append(jnp.concatenate([hi, plain - hi], axis=0))
        left = jnp.concatenate(lefts, axis=1).astype(BF)
        span = slice(first * PTS, (first + len(blocks)) * PTS)
        upper = dot_nt(left, cact[0, :, span])
        lower = dot_nt(left, cact[1, :, span])
        sums = [upper[0:8] + upper[8:16] + lower[0:8]]
        ones = jnp.ones((16, PTS), BF)
        for ref, powers in ((cone, 0), (ccurve, 1)):
            weighted = None
            for k, (weight, _, conductivity) in enumerate(blocks):
                factor = weight * conductivity if powers else weight
                term = ref[:, (first + k) * PTS : (first + k + 1) * PTS] * factor
                weighted = term if weighted is None else weighted + term
            hi, lo = split2(weighted)
            sums.append((dot_nt(ones, hi) + dot_nt(ones, lo))[0:8])
        return sums

    blocks = []
    for j in range(NETS):
        x = xs[j, 0]
        v = coarse_inputs(j, x)
        base = eown[j, 0:1, :] + coarse_forward(j, v, x[4:5], True) - source[j : j + 1, :]
        eown[j, 0:1, :] = base
        blocks.append((base * (1.0 / PTS), v, x[4:5]))
    own_sums = coarse_sums(blocks, 0)
    for k in range(3):
        csums[k] = own_sums[k]


    arrive(*g_args)
    hear(0)
    pass_on(1)
    def choose(parts):
        picked = parts[-1]
        for k in range(len(parts) - 2, -1, -1):
            picked = jnp.where(group == k, parts[k], picked)
        return picked

    blank = jnp.zeros((8, PTS), F32)
    for n in range(NETS):
        b, c = n // 2, n % 2
        slots = [
            gin[0, n],
            gin[1, n],
            gbuf[0, n + 2] if b == 0 else gin[2, n - 2],
            gbuf[0, n - 2] if b == 1 else gin[3, n + 2],
        ]
        xs[n, 1] = choose(slots)
        slots = [
            gbuf[1, n + 1] if c == 0 else gin[4, n - 1],
            gbuf[1, n - 1] if c == 1 else gin[5, n + 1],
            blank,
        ]
        xs[n, 2] = choose(slots)

    def joined_halves(first, second):
        return jnp.where(lane < HID, first, pltpu.roll(second, HID, 1))

    def face_block(n, tile):
        x = xs[n, tile]
        return coarse_inputs(n, x), x[4:5]

    face_blocks = [face_block(n, 1) for n in range(NETS)]
    for n in range(0, NETS, 2):
        face_blocks.append(
            tuple(map(joined_halves, face_block(n, 2), face_block(n + 1, 2)))
        )
    for k, (v, level) in enumerate(face_blocks):
        coarse_forward(NETS + k, v, level, False)

    def face_forward(n, carry):
        first, second = forward(n, (1, 2))
        ebuf[0, pl.ds(n, 1), :] = first
        ebuf[1, pl.ds(n, 1), :] = second
        return carry

    ebuf[...] = jnp.zeros_like(ebuf)
    lax.fori_loop(0, NETS, face_forward, 0, unroll=4)
    e_args = (lambda slot: ebuf.at[slot // 4], ein, e_send, e_recv, True)
    exchange(*e_args)

    weights = [
        [
            ebuf[tile, n : n + 1, :] * xs[n, tile + 1, 5:6, :] * (1.0 / PTS)
            for tile in range(2)
        ]
        for n in range(NETS)
    ]
    weights = [pair[0] for pair in weights] + [
        joined_halves(weights[n][1], weights[n + 1][1]) for n in range(0, NETS, 2)
    ]
    blocks = [(weight, v, level) for weight, (v, level) in zip(weights, face_blocks)]
    sums = [csums[k] + part for k, part in enumerate(coarse_sums(blocks, NETS))]
    moments, s_one, s_curve = sums[0][0:5], sums[1][0:1], sums[2][0:1]
    extra = jnp.concatenate(
        [
            (4.0 * scales[0] * scales[0]) * ci[0:1] * co * s_curve,
            (4.0 * scales[1] * scales[1]) * ci[1:2] * co * s_curve,
            (4.0 * scales[2] * scales[2]) * ci[2:3] * co * s_curve,
            2.0 * co * s_one,
            jnp.zeros((1, COARSE), F32),
        ],
        axis=0,
    )
    outer_grad = 2.0 * ci[3:4] * s_one + 2.0 * squares * s_curve
    partial_sums = jnp.concatenate([moments + extra, outer_grad], axis=0)
    ar_start(
        0,
        jnp.concatenate([partial_sums[:, k * PTS : (k + 1) * PTS] for k in range(4)], axis=0),
    )

    hear(1)
    pass_on(2)

    arrive(*e_args)
    for j in range(NETS):
        b, c = j // 2, j % 2

        def row(ref, k):
            return ref[k : k + 1, :]

        first = choose(
            [
                row(ein.at[0], j),
                row(ein.at[1], j),
                row(ebuf.at[0], j - 2) if b == 1 else row(ein.at[2], j + 2),
                row(ebuf.at[0], j + 2) if b == 0 else row(ein.at[3], j - 2),
            ]
        )
        second = choose(
            [
                row(ebuf.at[1], j - 1) if c == 1 else row(ein.at[4], j + 1),
                row(ebuf.at[1], j + 1) if c == 0 else row(ein.at[5], j - 1),
                jnp.zeros((1, PTS), F32),
            ]
        )
        spread = dot_nt(stacked3(jnp.concatenate([first, second], axis=1)), hot[j])
        residual = eown[j, 0:1, :] + spread[0:1] + spread[1:2] + spread[2:3]
        res_out[j : j + 1, :] = residual
        scaled = residual * (1.0 / PTS)
        eown[j] = jnp.broadcast_to(scaled, (8, PTS))
        moved = dot(stacked3(scaled), hot[j])
        moved = moved[0:1] + moved[1:2] + moved[2:3]
        rbuf[0, j : j + 1, :] = moved[:, 0:PTS]
        rbuf[1, j : j + 1, :] = moved[:, PTS : 2 * PTS]
    rbuf[:, 4:8, :] = jnp.zeros((2, 4, PTS), F32)
    r_args = (lambda slot: rbuf.at[slot // 4], rin, r_send, r_recv, False)
    exchange(*r_args)

    hear(2)
    ar_start(1, ar_finish(0))

    def own_backward(n, carry):
        backward(n, (0,), [eown[n, 0:1, :]], False)
        return carry

    lax.fori_loop(0, NETS, own_backward, 0, unroll=4)

    arrive(*r_args)
    for n in range(NETS):
        b, c = n // 2, n % 2
        second = choose(
            [
                rbuf[1, n + 1 : n + 2, :] if c == 0 else rin[4, n - 1 : n, :],
                rbuf[1, n - 1 : n, :] if c == 1 else rin[5, n + 1 : n + 2, :],
                jnp.zeros((1, PTS), F32),
            ]
        )
        cols[n, 1] = jnp.broadcast_to(second, (8, PTS))

        first = choose(
            [
                rin[0, n : n + 1, :],
                rin[1, n : n + 1, :],
                rbuf[0, n + 2 : n + 3, :] if b == 0 else rin[2, n - 2 : n - 1, :],
                rbuf[0, n - 2 : n - 1, :] if b == 1 else rin[3, n + 2 : n + 3, :],
            ]
        )
        cols[n, 0] = jnp.broadcast_to(first, (8, PTS))

    def face_backward(n, carry):
        backward(n, (1, 2), [cols[n, 0, 0:1, :], cols[n, 1, 0:1, :]], True)
        joined = []
        for ref in (acc2, acc3):
            low_rows = ref[n, 0:64, :]
            high_rows = ref[n, 64:128, :]
            joined.append(low_rows[:, 0:64] + high_rows[:, 0:64] + high_rows[:, 64:128])
        work[n] = jnp.concatenate(joined, axis=1)
        even = work[n, pl.ds(0, 32, stride=2), :]
        odd = work[n, pl.ds(1, 32, stride=2), :]
        bias2 = acc2[n, 128:129, :]
        bias3 = acc3[n, 128:129, :]
        bias2 = bias2[:, 0:64] + bias2[:, 64:128]
        bias3 = bias3[:, 0:64] + bias3[:, 64:128]
        first = acc1[n, 0:8, :] + acc1[n, 8:16, :]
        first = first[:, 0:64] + first[:, 64:128]
        last = acco[n, 0:1, :] + acco[n, 1:2, :] + acco[n, 2:3, :]
        last = last[:, 0:64] + last[:, 64:128]
        flat_out[n, 0:1, 0:64] = first[0:1]
        flat_out[n, 0:1, 64:128] = first[1:2]
        flat_out[n, 1:2, 0:64] = first[2:3]
        flat_out[n, 1:2, 64:128] = first[3:4]
        flat_out[n, 2:3, 0:64] = first[4:5]
        flat_out[n, 2:34, 64:128] = even[:, 0:64]
        flat_out[n, 3:35, 0:64] = odd[:, 0:64]
        flat_out[n, 34:35, 64:128] = bias2
        flat_out[n, 35:67, 0:64] = even[:, 64:128]
        flat_out[n, 35:67, 64:128] = odd[:, 64:128]
        flat_out[n, 67:68, 0:64] = bias3
        flat_out[n, 67:68, 64:128] = last
        return carry

    lax.fori_loop(0, NETS, face_backward, 0, unroll=4)
    count = NETS * sizes[0] * sizes[1] * sizes[2]
    for n in range(NETS):
        grad_out[n // 2, :, n % 2, :] = flat_out[n]
    stores = [
        pltpu.make_async_copy(near, away, out_sem.at[k])
        for k, (near, away) in enumerate(
            (
                (res_out, res_far),
                (grad_out, grad_far),
                (inner_out, inner_far),
                (outer_out, outer_far),
            )
        )
    ]
    stores[0].start()
    stores[1].start()
    for args in (g_args, e_args, r_args):
        sent(*args)
    total = ar_finish(1) * (count ** (-0.5))
    for k in range(4):
        inner_out[:, k * PTS : (k + 1) * PTS] = total[6 * k : 6 * k + 5]
        outer_out[:, k * PTS : (k + 1) * PTS] = total[6 * k + 5 : 6 * k + 6]
    stores[2].start()
    stores[3].start()
    for store in stores:
        store.wait()
    for stage in range(2):
        for out in ar_copies(stage, False):
            out.wait_send()


def writer(*refs):
    for k in range(4):
        refs[k + 4][...] = refs[k][...]


def on_device(fine_params, coarse_inner, coarse_outer, points, source, conductivity, face_points):
    sizes = tuple(lax.axis_size(axis) for axis in AXES)
    far = pl.BlockSpec(memory_space=pltpu.HBM)
    results = pl.pallas_call(
        partial(kernel, sizes),
        out_shape=(
            jax.ShapeDtypeStruct((NETS, PTS), F32),
            jax.ShapeDtypeStruct((2, ROWS, 2, PTS), F32),
            jax.ShapeDtypeStruct((5, COARSE), F32),
            jax.ShapeDtypeStruct((1, COARSE), F32),
        ),
        in_specs=[far] * 7,
        out_specs=(far,) * 4,
        scratch_shapes=[
            pltpu.VMEM((NETS, PTS), F32),
            pltpu.VMEM((2, ROWS, 2, PTS), F32),
            pltpu.VMEM((5, COARSE), F32),
            pltpu.VMEM((1, COARSE), F32),
            pltpu.SemaphoreType.DMA((4,)),
            pltpu.VMEM((2, ROWS, 2, PTS), F32),
            pltpu.VMEM((5, COARSE), F32),
            pltpu.VMEM((1, COARSE), F32),
            pltpu.VMEM((NETS, 4, PTS), F32),
            pltpu.VMEM((NETS, PTS), F32),
            pltpu.VMEM((2, 2), F32),
            pltpu.VMEM((2, 6, 2, FACE), jnp.int32),
            pltpu.SemaphoreType.DMA((7,)),
            pltpu.VMEM((NETS, PTS, 2 * PTS), BF),
            pltpu.VMEM((2, NETS, 8, PTS), F32),
            pltpu.VMEM((6, NETS, 8, PTS), F32),
            pltpu.VMEM((2, 8, PTS), F32),
            pltpu.VMEM((6, 8, PTS), F32),
            pltpu.VMEM((2, 8, PTS), F32),
            pltpu.VMEM((6, 8, PTS), F32),
            pltpu.VMEM((NETS, 3, 8, PTS), F32),
            pltpu.VMEM((NETS, 2, 8, PTS), F32),
            pltpu.VMEM((NETS, 8, HID, PTS), F32),
            pltpu.VMEM((NETS, HID, PTS), F32),
            pltpu.VMEM((NETS, 2, HID, 3 * HID), BF),
            pltpu.VMEM((NETS, 2, HID, 3 * HID), BF),
            pltpu.VMEM((NETS, 208, 3 * WIDTH), BF),
            pltpu.VMEM((NETS, 208, 3 * WIDTH), BF),
            pltpu.VMEM((NETS, HID, 3 * PTS), F32),
            pltpu.VMEM((NETS, HID, 3 * WIDTH), F32),
            pltpu.VMEM((NETS, HID, 3 * WIDTH), F32),
            pltpu.VMEM((NETS, PTS, 3 * PTS), BF),
            pltpu.VMEM((3 * NETS, 192, 3 * WIDTH), BF),
            pltpu.VMEM((NETS, 144, PTS), F32),
            pltpu.VMEM((NETS, 144, PTS), F32),
            pltpu.VMEM((NETS, 16, PTS), F32),
            pltpu.VMEM((NETS, 16, PTS), F32),
            pltpu.VMEM((NETS, HID, PTS), F32),
            pltpu.VMEM((NETS, 8, PTS), F32),
            pltpu.VMEM((3, COARSE, PTS), F32),
            pltpu.VMEM((2, COARSE, 10 * PTS), BF),
            pltpu.VMEM((COARSE, 10 * PTS), F32),
            pltpu.VMEM((COARSE, 10 * PTS), F32),
            pltpu.VMEM((3, 8, COARSE), F32),
            pltpu.VMEM((2, 16, 24, PTS), F32),
            pltpu.SemaphoreType.DMA((6,)),
            pltpu.SemaphoreType.DMA((6,)),
            pltpu.SemaphoreType.DMA((6,)),
            pltpu.SemaphoreType.DMA((6,)),
            pltpu.SemaphoreType.DMA((6,)),
            pltpu.SemaphoreType.DMA((6,)),
            pltpu.SemaphoreType.DMA((2, 16)),
            pltpu.SemaphoreType.DMA((2, 16)),
            pltpu.SemaphoreType.REGULAR((3, 2)),
            pltpu.VMEM((NETS, ROWS, PTS), F32),
        ],
        compiler_params=pltpu.CompilerParams(
            collective_id=0, has_side_effects=True, vmem_limit_bytes=63 * 1024 * 1024
        ),
    )(
        fine_params.reshape(2, 2, ROWS, PTS).transpose(0, 2, 1, 3),
        coarse_inner,
        coarse_outer.reshape(1, COARSE),
        points.reshape(NETS, 4, PTS),
        source.reshape(NETS, PTS),
        conductivity.reshape(2, 2),
        face_points.transpose(0, 1, 3, 2, 4).reshape(2, 6, 2, FACE),
    )
    residual, grads, inner_grads, outer_grads = pl.pallas_call(
        writer,
        out_shape=tuple(jax.ShapeDtypeStruct(value.shape, F32) for value in results),
        in_specs=[pl.BlockSpec(memory_space=pltpu.VMEM)] * 4,
        out_specs=(pl.BlockSpec(memory_space=pltpu.VMEM),) * 4,
        compiler_params=pltpu.CompilerParams(vmem_limit_bytes=63 * 1024 * 1024),
    )(*results)
    return (
        residual.reshape(source.shape),
        grads.transpose(0, 2, 1, 3).reshape(fine_params.shape),
        inner_grads,
        outer_grads.reshape(COARSE),
    )


def solution(mesh):
    return jax.shard_map(
        on_device,
        mesh=mesh,
        in_specs=(
            P("gx", "gy", "gz", None),
            P(),
            P(),
            P("gx", "gy", "gz", None, None),
            P("gx", "gy", "gz", None),
            P("gx", "gy", "gz"),
            P("gx", "gy", "gz", None, None),
        ),
        out_specs=(P("gx", "gy", "gz", None), P("gx", "gy", "gz", None), P(), P()),
        check_vma=False,
    )
```

```python
from functools import partial

import jax
import jax.numpy as jnp
from jax import lax
from jax.experimental import pallas as pl
from jax.experimental.pallas import tpu as pltpu
from jax.sharding import PartitionSpec as P

PTS = 128
FACE = 32
HID = 64
COARSE = 512
ROWS = 68
NETS = 4
CH = 6
WIDTH = CH * PTS
AXES = ("gx", "gy", "gz")
MESH = pl.DeviceIdType.MESH
BF = jnp.bfloat16
F32 = jnp.float32


def split2(x):
    hi = x.astype(BF)
    return hi, (x - hi.astype(F32)).astype(BF)


def split3(x):
    hi = x.astype(BF)
    rest = x - hi.astype(F32)
    mid = rest.astype(BF)
    return hi, mid, (rest - mid.astype(F32)).astype(BF)


def dot(a, b):
    return lax.dot_general(a, b, (((1,), (0,)), ((), ())), preferred_element_type=F32)


def dot_nt(a, b):
    return lax.dot_general(a, b, (((1,), (1,)), ((), ())), preferred_element_type=F32)


def iota(shape, dim):
    return lax.broadcasted_iota(jnp.int32, shape, dim)


def stacked3(row):
    which = iota((16, row.shape[1]), 0)
    hi = row.astype(BF).astype(F32)
    rest = row - hi
    mid = rest.astype(BF).astype(F32)
    low = rest - mid
    rows = jnp.where(which == 0, hi, jnp.where(which == 1, mid, jnp.where(which == 2, low, 0.0)))
    return rows.astype(BF)


def coefficients(x):
    sx, sy, sz, kappa = x[0:1], x[1:2], x[2:3], x[4:5]
    square = sx * sx + sy * sy + sz * sz
    window = jnp.exp(-square)
    scaled = kappa * window
    return (
        scaled * (6.0 - 4.0 * square),
        4.0 * scaled * sx,
        4.0 * scaled * sy,
        4.0 * scaled * sz,
        2.0 * window,
        -scaled,
    )


def kernel(
    sizes,
    params_hbm,
    inner_hbm,
    outer_hbm,
    points_hbm,
    source_hbm,
    kappa_hbm,
    faces_hbm,
    res_far,
    grad_far,
    inner_far,
    outer_far,
    res_out,
    grad_out,
    inner_out,
    outer_out,
    out_sem,
    params,
    inner,
    outer,
    points,
    source,
    kappa,
    faces,
    in_sem,
    hot,
    gbuf,
    gin,
    ebuf,
    ein,
    rbuf,
    rin,
    xs,
    cols,
    wide,
    wsq,
    lf,
    lb,
    act1,
    act2,
    hid1,
    state2,
    state3,
    qs,
    dz,
    acc3,
    acc2,
    acc1,
    acco,
    work,
    eown,
    ccols,
    cact,
    cone,
    ccurve,
    csums,
    ar,
    g_send,
    g_recv,
    e_send,
    e_recv,
    r_send,
    r_recv,
    ar_send,
    ar_recv,
    tokens,
    flat_out,
):
    place = [lax.axis_index(axis) for axis in AXES]
    def target(slot, flip):
        axis = slot // 2
        sign = (2 * (slot % 2) - 1) * (-1 if flip else 1)
        return AXES[axis], place[axis] + sign, sizes[axis]

    groups = [
        (
            place[1] * sizes[2] + place[2],
            sizes[1] * sizes[2],
            lambda p: {"gy": p // sizes[2], "gz": lax.rem(p, sizes[2])},
        ),
        (place[0], sizes[0], lambda p: {"gx": p}),
    ]

    def partners(stage):
        pos, size, _ = groups[stage]
        if sizes != (16, 4, 4):
            return [lax.rem(pos + k, size) for k in range(1, size)]
        if stage == 1:
            steps = [(2 * a + min(z, 8 - z), a, z) for a in range(2) for z in range(8)]
            return [
                lax.rem(pos // 8 + a, 2) * 8 + lax.rem(pos + z, 8)
                for hops, a, z in sorted(steps, reverse=True)
                if hops
            ]
        steps = [
            (4 * a + 4 * min(y, 4 - y) + b, a, b, y)
            for a in range(2)
            for b in range(2)
            for y in range(4)
        ]
        return [
            lax.rem(place[1] // 2 + a, 2) * 8 + lax.rem(place[1] + b, 2) * 4 + lax.rem(place[2] + y, 4)
            for hops, a, b, y in sorted(steps, reverse=True)
            if hops
        ]

    def ring(axis, step):
        return {AXES[axis]: lax.rem(place[axis] + step + sizes[axis], sizes[axis])}

    def pass_on(level):
        for side in range(2):
            pl.semaphore_signal(
                tokens.at[level, side],
                inc=1,
                device_id=ring(0, (1 << level) if side else -(1 << level)),
                device_id_type=MESH,
            )

    def hear(level):
        for side in range(2):
            pl.semaphore_wait(tokens.at[level, side], 1)

    def exchange(source_of, landing, send_sem, recv_sem, flip):
        for slot in range(6):
            axis, where, size = target(slot, flip)

            @pl.when(jnp.logical_and(where >= 0, where < size))
            def _(slot=slot, axis=axis, where=where):
                pltpu.make_async_remote_copy(
                    source_of(slot), landing.at[slot], send_sem.at[slot], recv_sem.at[slot],
                    device_id={axis: where}, device_id_type=MESH,
                ).start()

    def arrive(source_of, landing, send_sem, recv_sem, flip):
        for slot in range(6):
            axis, where, size = target(slot, not flip)

            @pl.when(jnp.logical_and(where >= 0, where < size))
            def _(slot=slot, axis=axis, where=where):
                pltpu.make_async_remote_copy(
                    source_of(slot), landing.at[slot], send_sem.at[slot], recv_sem.at[slot],
                    device_id={axis: where}, device_id_type=MESH,
                ).wait_recv()

    def sent(source_of, landing, send_sem, recv_sem, flip):
        for slot in range(6):
            axis, where, size = target(slot, flip)

            @pl.when(jnp.logical_and(where >= 0, where < size))
            def _(slot=slot, axis=axis, where=where):
                pltpu.make_async_remote_copy(
                    source_of(slot), landing.at[slot], send_sem.at[slot], recv_sem.at[slot],
                    device_id={axis: where}, device_id_type=MESH,
                ).wait_send()

    def ar_copies(stage, arriving):
        pos, _, member = groups[stage]
        for partner in partners(stage):
            slot = partner if arriving else pos
            yield pltpu.make_async_remote_copy(
                ar.at[stage, pos], ar.at[stage, slot],
                ar_send.at[stage, partner], ar_recv.at[stage, slot],
                device_id=member(partner), device_id_type=MESH,
            )

    def ar_start(stage, value):
        ar[stage, groups[stage][0]] = value
        for out in ar_copies(stage, False):
            out.start()

    def ar_finish(stage):
        for back in ar_copies(stage, True):
            back.wait_recv()
        total = ar[stage, 0]
        for p in range(1, groups[stage][1]):
            total = total + ar[stage, p]
        return total

    fetches = [
        pltpu.make_async_copy(far, near, in_sem.at[k])
        for k, (far, near) in enumerate(
            (
                (points_hbm, points),
                (faces_hbm, faces),
                (kappa_hbm, kappa),
                (params_hbm, params),
                (inner_hbm, inner),
                (outer_hbm, outer),
                (source_hbm, source),
            )
        )
    ]
    for fetch in fetches:
        fetch.start()

    gin[...] = jnp.zeros_like(gin)
    ein[...] = jnp.zeros_like(ein)
    rin[...] = jnp.zeros_like(rin)

    barrier = pltpu.get_barrier_semaphore()
    for step in (-1, 1):
        pl.semaphore_signal(barrier, inc=1, device_id=ring(0, step), device_id_type=MESH)
    pos, size, member = groups[0]
    for k in range(1, size):
        pl.semaphore_signal(
            barrier, inc=1, device_id=member(lax.rem(pos + k, size)), device_id_type=MESH
        )

    lane = iota((1, PTS), 1)
    row8 = iota((8, PTS), 0)
    group = lane // FACE
    for fetch in fetches[0:3]:
        fetch.wait()
    for j in range(NETS):
        b, c = j // 2, j % 2
        index = [faces[b, k, c : c + 1, :] for k in range(6)]
        first = jnp.concatenate(index[0:4], axis=1)
        second = jnp.concatenate(index[4:6] + [jnp.full((1, 2 * FACE), -1, jnp.int32)], axis=1)
        point = iota((PTS, PTS), 0)
        hot[j, :, 0:PTS] = jnp.where(point == first, 1.0, 0.0).astype(BF)
        hot[j, :, PTS : 2 * PTS] = jnp.where(point == second, 1.0, 0.0).astype(BF)
        own = jnp.concatenate([points[j], jnp.zeros((4, PTS), F32)], axis=0)
        own = jnp.where(row8 == 4, kappa[b : b + 1, c : c + 1], own)
        own = jnp.where(row8 == 5, 1.0, own)
        xs[j, 0] = own
        hi, mid, low_part = split3(own)
        pieces = jnp.concatenate([hi, mid, low_part, jnp.zeros_like(hi)], axis=0)
        moved = dot(pieces, hot[j])
        moved = moved[0:8] + moved[8:16] + moved[16:24]
        shift_a = jnp.where(row8 == group // 2, (2 * (group % 2) - 1).astype(F32), 0.0)
        shift_b = jnp.where(row8 == 2, jnp.where(group < 2, (2 * (group % 2) - 1).astype(F32), 0.0), 0.0)
        gbuf[0, j] = moved[:, 0:PTS] - shift_a
        gbuf[1, j] = moved[:, PTS : 2 * PTS] - shift_b

    pl.semaphore_wait(barrier, 2 + groups[0][1] - 1)
    g_args = (lambda slot: gbuf.at[slot // 4], gin, g_send, g_recv, False)
    exchange(*g_args)
    pass_on(0)

    for fetch in fetches[3:]:
        fetch.wait()
    half = iota((32, PTS), 1) < HID
    for n in range(NETS):
        flat = params[n // 2, :, n % 2, :]
        even = pltpu.roll(jnp.where(half, flat[35:67], flat[2:34]), HID, 1)
        odd = jnp.where(half, flat[3:35], flat[35:67])
        work[n, pl.ds(0, 32, stride=2), :] = even
        work[n, pl.ds(1, 32, stride=2), :] = odd
        both = work[n]
        hi, lo = split2(both)
        lb[n, 0, :, 0:64] = hi[:, 0:64]
        lb[n, 0, :, 64:128] = hi[:, 0:64]
        lb[n, 0, :, 128:192] = lo[:, 0:64]
        lb[n, 1, :, 0:64] = hi[:, 64:128]
        lb[n, 1, :, 64:128] = hi[:, 64:128]
        lb[n, 1, :, 128:192] = lo[:, 64:128]
        hi, lo = split2(both.T)
        for layer in range(2):
            lf[n, layer, :, 0:64] = hi[64 * layer : 64 * layer + 64]
            lf[n, layer, :, 64:128] = hi[64 * layer : 64 * layer + 64]
            lf[n, layer, :, 128:192] = lo[64 * layer : 64 * layer + 64]
        vectors = jnp.concatenate(
            [
                flat[0:1],
                pltpu.roll(flat[0:1], HID, 1),
                flat[1:2],
                pltpu.roll(flat[1:2], HID, 1),
                flat[2:3],
                pltpu.roll(flat[34:35], HID, 1),
                flat[67:68],
                pltpu.roll(flat[67:68], HID, 1),
            ],
            axis=0,
        )
        columns = vectors.T
        for k in range(8):
            wide[n, k] = jnp.broadcast_to(columns[0:64, k : k + 1], (64, PTS))
        wsq[n] = wide[n, 0] * wide[n, 0] + wide[n, 1] * wide[n, 1] + wide[n, 2] * wide[n, 2]
        first_channel = jnp.where(
            jnp.logical_and(iota((16, PTS), 0) == 0, iota((16, PTS), 1) >= 0), 1.0, 0.0
        ).astype(BF)
        for tile in range(3):
            for k in range(CH):
                at = (tile * CH + k) * PTS
                value = first_channel if k == 0 else jnp.zeros_like(first_channel)
                act1[n, 192:208, at : at + PTS] = value
                act2[n, 192:208, at : at + PTS] = value

    def put(ref, n, at, value):
        hi, lo = split2(value)
        ref[n, 0:64, at : at + PTS] = hi
        ref[n, 64:128, at : at + PTS] = lo
        ref[n, 128:192, at : at + PTS] = hi

    def forward(n, tiles):
        begin, end = tiles[0] * WIDTH, (tiles[-1] + 1) * WIDTH
        for tile in tiles:
            x = xs[n, tile]
            pre = (
                wide[n, 4]
                + wide[n, 0] * x[0:1]
                + wide[n, 1] * x[1:2]
                + wide[n, 2] * x[2:3]
                + wide[n, 3] * x[3:4]
            )
            hidden = jnp.tanh(pre)
            one = 1.0 - hidden * hidden
            two = -2.0 * hidden * one
            hid1[n, :, tile * PTS : (tile + 1) * PTS] = hidden
            at = tile * WIDTH
            put(act1, n, at, hidden)
            for k in range(4):
                put(act1, n, at + (k + 1) * PTS, one * wide[n, k])
            put(act1, n, at + 5 * PTS, two * wsq[n])
        product = dot(lf[n, 0], act1[n, 0:192, begin:end])
        for tile in tiles:
            at = tile * WIDTH
            z = [product[:, at - begin + k * PTS : at - begin + (k + 1) * PTS] for k in range(CH)]
            hidden = jnp.tanh(z[0] + wide[n, 5])
            one = 1.0 - hidden * hidden
            two = -2.0 * hidden * one
            state2[n, :, at : at + PTS] = hidden
            for k in range(1, CH):
                state2[n, :, at + k * PTS : at + (k + 1) * PTS] = z[k]
            put(act2, n, at, hidden)
            for k in range(1, 5):
                put(act2, n, at + k * PTS, one * z[k])
            put(act2, n, at + 5 * PTS, two * (z[1] * z[1] + z[2] * z[2] + z[3] * z[3]) + one * z[5])
        product = dot(lf[n, 1], act2[n, 0:192, begin:end])
        results = []
        for tile in tiles:
            at = tile * WIDTH
            z = [product[:, at - begin + k * PTS : at - begin + (k + 1) * PTS] for k in range(CH)]
            coef = coefficients(xs[n, tile])
            hidden = jnp.tanh(z[0] + wide[n, 6])
            one = 1.0 - hidden * hidden
            two = -2.0 * hidden * one
            mixed = coef[5] * z[5]
            for k in range(1, 5):
                mixed = mixed + coef[k] * z[k]
            curved = coef[5] * (z[1] * z[1] + z[2] * z[2] + z[3] * z[3])
            q = coef[0] * hidden + one * mixed + two * curved
            state3[n, :, at : at + PTS] = hidden
            for k in range(1, 4):
                state3[n, :, at + k * PTS : at + (k + 1) * PTS] = z[k]
            state3[n, :, at + 4 * PTS : at + 5 * PTS] = mixed
            state3[n, :, at + 5 * PTS : at + 6 * PTS] = q
            results.append(jnp.sum(wide[n, 7] * q, axis=0, keepdims=True))
        return results

    def backward(n, tiles, rows, add):
        begin, end = tiles[0] * WIDTH, (tiles[-1] + 1) * WIDTH

        def collect(ref, value):
            ref[n] = ref[n] + value if add else value

        for tile, row in zip(tiles, rows):
            at = tile * WIDTH
            coef = [value * row for value in coefficients(xs[n, tile])]
            hidden, z1, z2, z3, mixed, q = (
                state3[n, :, at + k * PTS : at + (k + 1) * PTS] for k in range(CH)
            )
            hi, lo = split2(q)
            qs[n, 0:64, tile * PTS : (tile + 1) * PTS] = hi
            qs[n, 64:128, tile * PTS : (tile + 1) * PTS] = lo
            squared = hidden * hidden
            one = 1.0 - squared
            three = -2.0 * one * (1.0 - 3.0 * squared)
            out = wide[n, 7]
            one = out * one
            two = -2.0 * hidden * one
            curved = coef[5] * (z1 * z1 + z2 * z2 + z3 * z3)
            put(dz, 3 * n + 0, at, coef[0] * one + two * (mixed * row) + (out * three) * curved)
            twice = 2.0 * coef[5] * two
            for k, z in ((1, z1), (2, z2), (3, z3)):
                put(dz, 3 * n + 0, at + k * PTS, coef[k] * one + twice * z)
            put(dz, 3 * n + 0, at + 4 * PTS, coef[4] * one)
            put(dz, 3 * n + 0, at + 5 * PTS, coef[5] * one)
        product = dot(lb[n, 1], dz[3 * n + 0, 0:192, begin:end])
        collect(acc3, dot_nt(act2[n, 64:208, begin:end], dz[3 * n + 0, 0:128, begin:end]))
        row = jnp.concatenate(rows, axis=1)
        span = slice(tiles[0] * PTS, (tiles[-1] + 1) * PTS)
        collect(acco, dot_nt(stacked3(row), qs[n, :, span]))
        for tile in tiles:
            at = tile * WIDTH
            a = [product[:, at - begin + k * PTS : at - begin + (k + 1) * PTS] for k in range(CH)]
            z = [state2[n, :, at + k * PTS : at + (k + 1) * PTS] for k in range(CH)]
            squared = z[0] * z[0]
            one = 1.0 - squared
            two = -2.0 * z[0] * one
            three = -2.0 * one * (1.0 - 3.0 * squared)
            mixed = z[5] * a[5]
            for k in range(1, 5):
                mixed = mixed + z[k] * a[k]
            curved = (z[1] * z[1] + z[2] * z[2] + z[3] * z[3]) * a[5]
            put(dz, 3 * n + 1, at, one * a[0] + two * mixed + three * curved)
            twice = 2.0 * two * a[5]
            for k in range(1, 4):
                put(dz, 3 * n + 1, at + k * PTS, one * a[k] + twice * z[k])
            put(dz, 3 * n + 1, at + 4 * PTS, one * a[4])
            put(dz, 3 * n + 1, at + 5 * PTS, one * a[5])
        product = dot(lb[n, 0], dz[3 * n + 1, 0:192, begin:end])
        collect(acc2, dot_nt(act1[n, 64:208, begin:end], dz[3 * n + 1, 0:128, begin:end]))
        total = None
        for tile in tiles:
            at = tile * WIDTH
            a = [product[:, at - begin + k * PTS : at - begin + (k + 1) * PTS] for k in range(CH)]
            hidden = hid1[n, :, tile * PTS : (tile + 1) * PTS]
            squared = hidden * hidden
            one = 1.0 - squared
            two = -2.0 * hidden * one
            three = -2.0 * one * (1.0 - 3.0 * squared)
            mixed = wide[n, 0] * a[1]
            for k in range(1, 4):
                mixed = mixed + wide[n, k] * a[k + 1]
            twice = 2.0 * two * a[5]
            base = tile * WIDTH
            put(dz, 3 * n + 2, base, one * a[0] + two * mixed + three * (wsq[n] * a[5]))
            for k in range(3):
                put(dz, 3 * n + 2, base + (k + 1) * PTS, one * a[k + 1] + twice * wide[n, k])
            put(dz, 3 * n + 2, base + 4 * PTS, one * a[4])
            x = xs[n, tile]
            hi = x.astype(BF).astype(F32)
            top = jnp.where(row8 < 4, hi, jnp.where(row8 == 4, 1.0, 0.0))
            bottom = jnp.where(row8 < 4, x - hi, 0.0)
            pieces = [jnp.concatenate([top, bottom], axis=0)]
            for k in range(4):
                pieces.append(jnp.where(iota((16, PTS), 0) == k, 1.0, 0.0))
            left = jnp.concatenate(pieces, axis=1).astype(BF)
            part = dot_nt(left, dz[3 * n + 2, 0:128, base : base + 5 * PTS])
            total = part if total is None else total + part
        collect(acc1, total)

    def own_forward(n, carry):
        eown[n] = jnp.broadcast_to(forward(n, (0,))[0], (8, PTS))
        return carry

    lax.fori_loop(0, NETS, own_forward, 0, unroll=4)

    scales = (2.0 / sizes[0], 2.0 / (2 * sizes[1]), 2.0 / (2 * sizes[2]))
    ci = inner[...]
    co = outer[...]
    squares = (
        ci[0:1] * ci[0:1] * (scales[0] * scales[0])
        + ci[1:2] * ci[1:2] * (scales[1] * scales[1])
        + ci[2:3] * ci[2:3] * (scales[2] * scales[2])
    )
    pad = jnp.zeros((3, COARSE), F32)
    c8 = jnp.concatenate([ci, pad], axis=0)
    hi = c8.astype(BF).astype(F32)
    mid = (c8 - hi).astype(BF).astype(F32)
    lo = c8 - hi - mid
    fronts = jnp.concatenate([hi, hi, mid, hi, lo, mid], axis=0).T.astype(BF)
    two_rows = jnp.concatenate(
        [2.0 * co * ci[3:4], 2.0 * co * squares, jnp.zeros((6, COARSE), F32)], axis=0
    ).T
    ccols[0] = jnp.broadcast_to(two_rows[:, 0:1], (COARSE, PTS))
    ccols[1] = jnp.broadcast_to(two_rows[:, 1:2], (COARSE, PTS))
    ccols[2] = 2.0 * ccols[0]

    def coarse_inputs(n, x):
        b, c = n // 2, n % 2
        centres = (
            place[0].astype(F32) + 0.5,
            (2 * place[1] + b).astype(F32) + 0.5,
            (2 * place[2] + c).astype(F32) + 0.5,
        )
        v = jnp.where(row8 == 3, x, 0.0)
        for k in range(3):
            v = jnp.where(row8 == k, (centres[k] + x) * scales[k] - 1.0, v)
        return jnp.where(row8 == 4, 1.0, v)

    def coarse_forward(block, v, conductivity, wanted):
        hi = v.astype(BF).astype(F32)
        mid = (v - hi).astype(BF).astype(F32)
        lo = v - hi - mid
        backs = jnp.concatenate([hi, mid, hi, lo, hi, mid], axis=0).astype(BF)
        hidden = jnp.tanh(dot(fronts, backs))
        squared = hidden * hidden
        one = 1.0 - squared
        curve = one * hidden
        level = ccols[1] * conductivity
        slope = level * (one * (1.0 - 3.0 * squared)) - ccols[2] * curve
        at = slice(block * PTS, (block + 1) * PTS)
        cone[:, at] = one
        ccurve[:, at] = curve
        hi, lo = split2(slope)
        cact[0, :, at] = hi
        cact[1, :, at] = lo
        if wanted:
            return jnp.sum(ccols[0] * one + level * curve, axis=0, keepdims=True)

    def coarse_sums(blocks, first):
        lefts = []
        for weight, v, _ in blocks:
            plain = weight * v
            hi = plain.astype(BF).astype(F32)
            lefts.append(jnp.concatenate([hi, plain - hi], axis=0))
        left = jnp.concatenate(lefts, axis=1).astype(BF)
        span = slice(first * PTS, (first + len(blocks)) * PTS)
        upper = dot_nt(left, cact[0, :, span])
        lower = dot_nt(left, cact[1, :, span])
        sums = [upper[0:8] + upper[8:16] + lower[0:8]]
        ones = jnp.ones((16, PTS), BF)
        for ref, powers in ((cone, 0), (ccurve, 1)):
            weighted = None
            for k, (weight, _, conductivity) in enumerate(blocks):
                factor = weight * conductivity if powers else weight
                term = ref[:, (first + k) * PTS : (first + k + 1) * PTS] * factor
                weighted = term if weighted is None else weighted + term
            hi, lo = split2(weighted)
            sums.append((dot_nt(ones, hi) + dot_nt(ones, lo))[0:8])
        return sums

    blocks = []
    for j in range(NETS):
        x = xs[j, 0]
        v = coarse_inputs(j, x)
        base = eown[j, 0:1, :] + coarse_forward(j, v, x[4:5], True) - source[j : j + 1, :]
        eown[j, 0:1, :] = base
        blocks.append((base * (1.0 / PTS), v, x[4:5]))
    own_sums = coarse_sums(blocks, 0)
    for k in range(3):
        csums[k] = own_sums[k]


    arrive(*g_args)
    hear(0)
    pass_on(1)
    def choose(parts):
        picked = parts[-1]
        for k in range(len(parts) - 2, -1, -1):
            picked = jnp.where(group == k, parts[k], picked)
        return picked

    blank = jnp.zeros((8, PTS), F32)
    for n in range(NETS):
        b, c = n // 2, n % 2
        slots = [
            gin[0, n],
            gin[1, n],
            gbuf[0, n + 2] if b == 0 else gin[2, n - 2],
            gbuf[0, n - 2] if b == 1 else gin[3, n + 2],
        ]
        xs[n, 1] = choose(slots)
        slots = [
            gbuf[1, n + 1] if c == 0 else gin[4, n - 1],
            gbuf[1, n - 1] if c == 1 else gin[5, n + 1],
            blank,
        ]
        xs[n, 2] = choose(slots)

    def joined_halves(first, second):
        return jnp.where(lane < HID, first, pltpu.roll(second, HID, 1))

    def face_block(n, tile):
        x = xs[n, tile]
        return coarse_inputs(n, x), x[4:5]

    face_blocks = [face_block(n, 1) for n in range(NETS)]
    for n in range(0, NETS, 2):
        face_blocks.append(
            tuple(map(joined_halves, face_block(n, 2), face_block(n + 1, 2)))
        )
    for k, (v, level) in enumerate(face_blocks):
        coarse_forward(NETS + k, v, level, False)

    def face_forward(n, carry):
        first, second = forward(n, (1, 2))
        ebuf[0, pl.ds(n, 1), :] = first
        ebuf[1, pl.ds(n, 1), :] = second
        return carry

    ebuf[...] = jnp.zeros_like(ebuf)
    lax.fori_loop(0, NETS, face_forward, 0, unroll=4)
    e_args = (lambda slot: ebuf.at[slot // 4], ein, e_send, e_recv, True)
    exchange(*e_args)

    weights = [
        [
            ebuf[tile, n : n + 1, :] * xs[n, tile + 1, 5:6, :] * (1.0 / PTS)
            for tile in range(2)
        ]
        for n in range(NETS)
    ]
    weights = [pair[0] for pair in weights] + [
        joined_halves(weights[n][1], weights[n + 1][1]) for n in range(0, NETS, 2)
    ]
    blocks = [(weight, v, level) for weight, (v, level) in zip(weights, face_blocks)]
    sums = [csums[k] + part for k, part in enumerate(coarse_sums(blocks, NETS))]
    moments, s_one, s_curve = sums[0][0:5], sums[1][0:1], sums[2][0:1]
    extra = jnp.concatenate(
        [
            (4.0 * scales[0] * scales[0]) * ci[0:1] * co * s_curve,
            (4.0 * scales[1] * scales[1]) * ci[1:2] * co * s_curve,
            (4.0 * scales[2] * scales[2]) * ci[2:3] * co * s_curve,
            2.0 * co * s_one,
            jnp.zeros((1, COARSE), F32),
        ],
        axis=0,
    )
    outer_grad = 2.0 * ci[3:4] * s_one + 2.0 * squares * s_curve
    partial_sums = jnp.concatenate([moments + extra, outer_grad], axis=0)
    ar_start(
        0,
        jnp.concatenate([partial_sums[:, k * PTS : (k + 1) * PTS] for k in range(4)], axis=0),
    )

    hear(1)
    pass_on(2)

    arrive(*e_args)
    for j in range(NETS):
        b, c = j // 2, j % 2

        def row(ref, k):
            return ref[k : k + 1, :]

        first = choose(
            [
                row(ein.at[0], j),
                row(ein.at[1], j),
                row(ebuf.at[0], j - 2) if b == 1 else row(ein.at[2], j + 2),
                row(ebuf.at[0], j + 2) if b == 0 else row(ein.at[3], j - 2),
            ]
        )
        second = choose(
            [
                row(ebuf.at[1], j - 1) if c == 1 else row(ein.at[4], j + 1),
                row(ebuf.at[1], j + 1) if c == 0 else row(ein.at[5], j - 1),
                jnp.zeros((1, PTS), F32),
            ]
        )
        spread = dot_nt(stacked3(jnp.concatenate([first, second], axis=1)), hot[j])
        residual = eown[j, 0:1, :] + spread[0:1] + spread[1:2] + spread[2:3]
        res_out[j : j + 1, :] = residual
        scaled = residual * (1.0 / PTS)
        eown[j] = jnp.broadcast_to(scaled, (8, PTS))
        moved = dot(stacked3(scaled), hot[j])
        moved = moved[0:1] + moved[1:2] + moved[2:3]
        rbuf[0, j : j + 1, :] = moved[:, 0:PTS]
        rbuf[1, j : j + 1, :] = moved[:, PTS : 2 * PTS]
    rbuf[:, 4:8, :] = jnp.zeros((2, 4, PTS), F32)
    r_args = (lambda slot: rbuf.at[slot // 4], rin, r_send, r_recv, False)
    exchange(*r_args)

    hear(2)
    ar_start(1, ar_finish(0))

    def own_backward(n, carry):
        backward(n, (0,), [eown[n, 0:1, :]], False)
        return carry

    lax.fori_loop(0, NETS, own_backward, 0, unroll=4)

    arrive(*r_args)
    for n in range(NETS):
        b, c = n // 2, n % 2
        second = choose(
            [
                rbuf[1, n + 1 : n + 2, :] if c == 0 else rin[4, n - 1 : n, :],
                rbuf[1, n - 1 : n, :] if c == 1 else rin[5, n + 1 : n + 2, :],
                jnp.zeros((1, PTS), F32),
            ]
        )
        cols[n, 1] = jnp.broadcast_to(second, (8, PTS))

        first = choose(
            [
                rin[0, n : n + 1, :],
                rin[1, n : n + 1, :],
                rbuf[0, n + 2 : n + 3, :] if b == 0 else rin[2, n - 2 : n - 1, :],
                rbuf[0, n - 2 : n - 1, :] if b == 1 else rin[3, n + 2 : n + 3, :],
            ]
        )
        cols[n, 0] = jnp.broadcast_to(first, (8, PTS))

    def face_backward(n, carry):
        backward(n, (1, 2), [cols[n, 0, 0:1, :], cols[n, 1, 0:1, :]], True)
        joined = []
        for ref in (acc2, acc3):
            low_rows = ref[n, 0:64, :]
            high_rows = ref[n, 64:128, :]
            joined.append(low_rows[:, 0:64] + high_rows[:, 0:64] + high_rows[:, 64:128])
        work[n] = jnp.concatenate(joined, axis=1)
        even = work[n, pl.ds(0, 32, stride=2), :]
        odd = work[n, pl.ds(1, 32, stride=2), :]
        bias2 = acc2[n, 128:129, :]
        bias3 = acc3[n, 128:129, :]
        bias2 = bias2[:, 0:64] + bias2[:, 64:128]
        bias3 = bias3[:, 0:64] + bias3[:, 64:128]
        first = acc1[n, 0:8, :] + acc1[n, 8:16, :]
        first = first[:, 0:64] + first[:, 64:128]
        last = acco[n, 0:1, :] + acco[n, 1:2, :] + acco[n, 2:3, :]
        last = last[:, 0:64] + last[:, 64:128]
        flat_out[n, 0:1, 0:64] = first[0:1]
        flat_out[n, 0:1, 64:128] = first[1:2]
        flat_out[n, 1:2, 0:64] = first[2:3]
        flat_out[n, 1:2, 64:128] = first[3:4]
        flat_out[n, 2:3, 0:64] = first[4:5]
        flat_out[n, 2:34, 64:128] = even[:, 0:64]
        flat_out[n, 3:35, 0:64] = odd[:, 0:64]
        flat_out[n, 34:35, 64:128] = bias2
        flat_out[n, 35:67, 0:64] = even[:, 64:128]
        flat_out[n, 35:67, 64:128] = odd[:, 64:128]
        flat_out[n, 67:68, 0:64] = bias3
        flat_out[n, 67:68, 64:128] = last
        return carry

    lax.fori_loop(0, NETS, face_backward, 0, unroll=4)
    count = NETS * sizes[0] * sizes[1] * sizes[2]
    stores = [
        pltpu.make_async_copy(near, away, out_sem.at[k])
        for k, (near, away) in enumerate(
            (
                (res_out, res_far),
                (grad_out.at[0], grad_far.at[0]),
                (grad_out.at[1], grad_far.at[1]),
                (inner_out, inner_far),
                (outer_out, outer_far),
            )
        )
    ]
    stores[0].start()
    for b in range(2):
        for c in range(2):
            grad_out[b, :, c, :] = flat_out[2 * b + c]
        stores[1 + b].start()
    for args in (g_args, e_args, r_args):
        sent(*args)
    total = ar_finish(1) * (count ** (-0.5))
    for k in range(4):
        inner_out[:, k * PTS : (k + 1) * PTS] = total[6 * k : 6 * k + 5]
        outer_out[:, k * PTS : (k + 1) * PTS] = total[6 * k + 5 : 6 * k + 6]
    stores[3].start()
    stores[4].start()
    for store in stores:
        store.wait()
    for stage in range(2):
        for out in ar_copies(stage, False):
            out.wait_send()


def writer(*refs):
    for k in range(4):
        refs[k + 4][...] = refs[k][...]


def on_device(fine_params, coarse_inner, coarse_outer, points, source, conductivity, face_points):
    sizes = tuple(lax.axis_size(axis) for axis in AXES)
    far = pl.BlockSpec(memory_space=pltpu.HBM)
    results = pl.pallas_call(
        partial(kernel, sizes),
        out_shape=(
            jax.ShapeDtypeStruct((NETS, PTS), F32),
            jax.ShapeDtypeStruct((2, ROWS, 2, PTS), F32),
            jax.ShapeDtypeStruct((5, COARSE), F32),
            jax.ShapeDtypeStruct((1, COARSE), F32),
        ),
        in_specs=[far] * 7,
        out_specs=(far,) * 4,
        scratch_shapes=[
            pltpu.VMEM((NETS, PTS), F32),
            pltpu.VMEM((2, ROWS, 2, PTS), F32),
            pltpu.VMEM((5, COARSE), F32),
            pltpu.VMEM((1, COARSE), F32),
            pltpu.SemaphoreType.DMA((5,)),
            pltpu.VMEM((2, ROWS, 2, PTS), F32),
            pltpu.VMEM((5, COARSE), F32),
            pltpu.VMEM((1, COARSE), F32),
            pltpu.VMEM((NETS, 4, PTS), F32),
            pltpu.VMEM((NETS, PTS), F32),
            pltpu.VMEM((2, 2), F32),
            pltpu.VMEM((2, 6, 2, FACE), jnp.int32),
            pltpu.SemaphoreType.DMA((7,)),
            pltpu.VMEM((NETS, PTS, 2 * PTS), BF),
            pltpu.VMEM((2, NETS, 8, PTS), F32),
            pltpu.VMEM((6, NETS, 8, PTS), F32),
            pltpu.VMEM((2, 8, PTS), F32),
            pltpu.VMEM((6, 8, PTS), F32),
            pltpu.VMEM((2, 8, PTS), F32),
            pltpu.VMEM((6, 8, PTS), F32),
            pltpu.VMEM((NETS, 3, 8, PTS), F32),
            pltpu.VMEM((NETS, 2, 8, PTS), F32),
            pltpu.VMEM((NETS, 8, HID, PTS), F32),
            pltpu.VMEM((NETS, HID, PTS), F32),
            pltpu.VMEM((NETS, 2, HID, 3 * HID), BF),
            pltpu.VMEM((NETS, 2, HID, 3 * HID), BF),
            pltpu.VMEM((NETS, 208, 3 * WIDTH), BF),
            pltpu.VMEM((NETS, 208, 3 * WIDTH), BF),
            pltpu.VMEM((NETS, HID, 3 * PTS), F32),
            pltpu.VMEM((NETS, HID, 3 * WIDTH), F32),
            pltpu.VMEM((NETS, HID, 3 * WIDTH), F32),
            pltpu.VMEM((NETS, PTS, 3 * PTS), BF),
            pltpu.VMEM((3 * NETS, 192, 3 * WIDTH), BF),
            pltpu.VMEM((NETS, 144, PTS), F32),
            pltpu.VMEM((NETS, 144, PTS), F32),
            pltpu.VMEM((NETS, 16, PTS), F32),
            pltpu.VMEM((NETS, 16, PTS), F32),
            pltpu.VMEM((NETS, HID, PTS), F32),
            pltpu.VMEM((NETS, 8, PTS), F32),
            pltpu.VMEM((3, COARSE, PTS), F32),
            pltpu.VMEM((2, COARSE, 10 * PTS), BF),
            pltpu.VMEM((COARSE, 10 * PTS), F32),
            pltpu.VMEM((COARSE, 10 * PTS), F32),
            pltpu.VMEM((3, 8, COARSE), F32),
            pltpu.VMEM((2, 16, 24, PTS), F32),
            pltpu.SemaphoreType.DMA((6,)),
            pltpu.SemaphoreType.DMA((6,)),
            pltpu.SemaphoreType.DMA((6,)),
            pltpu.SemaphoreType.DMA((6,)),
            pltpu.SemaphoreType.DMA((6,)),
            pltpu.SemaphoreType.DMA((6,)),
            pltpu.SemaphoreType.DMA((2, 16)),
            pltpu.SemaphoreType.DMA((2, 16)),
            pltpu.SemaphoreType.REGULAR((3, 2)),
            pltpu.VMEM((NETS, ROWS, PTS), F32),
        ],
        compiler_params=pltpu.CompilerParams(
            collective_id=0, has_side_effects=True, vmem_limit_bytes=63 * 1024 * 1024
        ),
    )(
        fine_params.reshape(2, 2, ROWS, PTS).transpose(0, 2, 1, 3),
        coarse_inner,
        coarse_outer.reshape(1, COARSE),
        points.reshape(NETS, 4, PTS),
        source.reshape(NETS, PTS),
        conductivity.reshape(2, 2),
        face_points.transpose(0, 1, 3, 2, 4).reshape(2, 6, 2, FACE),
    )
    residual, grads, inner_grads, outer_grads = pl.pallas_call(
        writer,
        out_shape=tuple(jax.ShapeDtypeStruct(value.shape, F32) for value in results),
        in_specs=[pl.BlockSpec(memory_space=pltpu.VMEM)] * 4,
        out_specs=(pl.BlockSpec(memory_space=pltpu.VMEM),) * 4,
        compiler_params=pltpu.CompilerParams(vmem_limit_bytes=63 * 1024 * 1024),
    )(*results)
    return (
        residual.reshape(source.shape),
        grads.transpose(0, 2, 1, 3).reshape(fine_params.shape),
        inner_grads,
        outer_grads.reshape(COARSE),
    )


def solution(mesh):
    return jax.shard_map(
        on_device,
        mesh=mesh,
        in_specs=(
            P("gx", "gy", "gz", None),
            P(),
            P(),
            P("gx", "gy", "gz", None, None),
            P("gx", "gy", "gz", None),
            P("gx", "gy", "gz"),
            P("gx", "gy", "gz", None, None),
        ),
        out_specs=(P("gx", "gy", "gz", None), P("gx", "gy", "gz", None), P(), P()),
        check_vma=False,
    )
```
